512 devices in a mesh: dp: 32 (over y, x), tensor: 16 (over z, core).
Axes of the slice: x: 4, y: 8, z: 8, core: 2. Of those that a mesh axis runs over, the one named last changes fastest.
Arguments:
- inputs: bfloat16 [4096, 8192], P('tensor', 'dp'), may hold values from -0.59765625 to 0.59765625
- cotangent: bfloat16 [4096, 8192], P('tensor', 'dp'), may hold values from -12288 to 12288
- queries: bfloat16 [4096, 4096], P('dp', 'tensor'), may hold values from -4.5 to 4.5
- key_rows: bfloat16 [4096, 512], P('dp'), may hold values from -4.5 to 4.5
- values: bfloat16 [4096, 512], P('dp'), may hold values from -6 to 6
- lengths: int32 [32, 8], P('dp'), may hold values from 1 to 64, as said below
- loss_counts: int32 [32], P('dp'), may hold values from 21 to 128
- query_weight: bfloat16 [8192, 4096], P('dp', 'tensor'), may hold values from -0.0625 to 0.0625
- key_weight: bfloat16 [8192, 512], P('dp', 'tensor'), may hold values from -0.0625 to 0.0625
- value_weight: bfloat16 [8192, 512], P('dp', 'tensor'), may hold values from -0.0625 to 0.0625
- output_weight: bfloat16 [4096, 8192], P('tensor', 'dp'), may hold values from -0.09375 to 0.09375
Outputs:
- input_gradient: bfloat16 [4096, 8192], P('tensor', 'dp')
- query_gradient: bfloat16 [8192, 4096], P('dp', 'tensor')
- key_gradient: bfloat16 [8192, 512], P('dp', 'tensor')
- value_gradient: bfloat16 [8192, 512], P('dp', 'tensor')
- output_gradient: bfloat16 [4096, 8192], P('tensor', 'dp')
The draws below stay inside these ranges and needn't reach their ends.
Inputs may be any that keep to these rules, and one draw needn't show every extreme that they name: Each row is one pack: 8 documents in order whose lengths sum to 128; the longest is exactly 64 tokens.
All inputs are finite; a program needn't handle non-finite values.
Results may differ from the reference program's by a relative error of at most 0.035.
Values may be sent and summed in bfloat16 or wider, within the bound.
A program may use at most 64 MiB of HBM per device.

```python
import jax
import jax.numpy as jnp
from jax import lax

D = 8192
H = 32
KVH = 4
HD = 128
TOK_DEV = 128
DOCS = 8
MOST = 64
TOKENS = 4096
N_DP = 32
N_TENSOR = 16


def pack_layout(key):
    key = jax.random.fold_in(key, 101)
    others = DOCS - 1
    spare_room = MOST - 1
    extra_units = TOK_DEV - MOST - others
    unit_owner = jnp.arange(others * spare_room, dtype=jnp.int32) // spare_room

    def one_row(row_key):
        perm_key, place_key = jax.random.split(row_key)
        chosen = jax.random.permutation(perm_key, unit_owner)[:extra_units]
        counts = jnp.sum((chosen[:, None] == jnp.arange(others, dtype=jnp.int32)[None, :]).astype(jnp.int32), axis=0) + 1
        long_place = jax.random.randint(place_key, (), 0, DOCS)
        slot_index = jnp.arange(DOCS, dtype=jnp.int32)
        shifted_up = jnp.take(counts, jnp.clip(slot_index, 0, others - 1))
        shifted_down = jnp.take(counts, jnp.clip(slot_index - 1, 0, others - 1))
        row_lengths = jnp.where(slot_index < long_place, shifted_up, jnp.where(slot_index == long_place, MOST, shifted_down))
        long_start = jnp.sum(jnp.where(slot_index < long_place, row_lengths, 0))
        return (row_lengths.astype(jnp.int32), long_start.astype(jnp.int32))
    row_keys = jax.random.split(key, N_DP)
    return jax.vmap(one_row)(row_keys)


def draw_lengths(key, part):
    row_lengths, long_start = pack_layout(key)
    return row_lengths


def draw_loss_counts(key, part):
    key = jax.random.fold_in(key, 7)
    place_index = jnp.arange(N_DP, dtype=jnp.int32)
    span_count = max(N_DP - 1, 1)
    lower_bound = TOK_DEV * (span_count + 2 * place_index) // (6 * span_count)
    upper_bound = TOK_DEV * (span_count + 2 * place_index) // (3 * span_count)
    raw_draw = jax.random.randint(key, (N_DP,), 0, 1 << 20)
    drawn = lower_bound + raw_draw % (upper_bound - lower_bound + 1)
    drawn = jnp.where(place_index == N_DP - 1, TOK_DEV, drawn)
    drawn = jnp.where(place_index == 0, TOK_DEV // 6, drawn)
    return drawn.astype(jnp.int32)


def draw_queries(key, part):
    key = jax.random.fold_in(key, 3)
    return jnp.clip(jax.random.normal(key, (TOKENS, H * HD), jnp.float32), -4.5, 4.5).astype(jnp.bfloat16)


def draw_key_rows(key, part):
    key = jax.random.fold_in(key, 5)
    return jnp.clip(jax.random.normal(key, (TOKENS, KVH * HD), jnp.float32), -4.5, 4.5).astype(jnp.bfloat16)


def steps_of(own_key, shape, pieces, least, largest):
    def one(position, blocks):
        heights = jax.random.uniform(jax.random.fold_in(jax.random.fold_in(own_key, 6), position), (blocks,), jnp.float32, least / len(pieces), largest / len(pieces))
        return jnp.repeat(jnp.exp(heights), shape[position] // blocks).reshape((-1,) + (1,) * (len(shape) - position - 1))

    level = one(*pieces[0])
    for cut in pieces[1:]:
        level = level * one(*cut)
    return level


def scatter_about(key, shape, deviation, limit, pieces=(), held_as=jnp.bfloat16):
    gain = steps_of(key, shape, pieces, -0.22, 0.18) if pieces else 1.0
    entries = jax.random.normal(key, shape, jnp.float32) * deviation * gain
    return jnp.minimum(jnp.maximum(entries, -limit), limit).astype(held_as)


def setup_inputs(seed: int = 0) -> dict:
    seeds = jax.random.split(jax.random.key(seed), 12)
    inputs = scatter_about(seeds[0], (TOKENS, D), 0.1, 0.59765625, ((0, 16), (1, 32)))
    cotangent = scatter_about(seeds[1], (TOKENS, D), (TOKENS / 2), 12288.0, ((0, 16), (1, 32)))
    queries = draw_queries(jax.random.fold_in(seeds[11], 71), 0)
    key_rows = draw_key_rows(jax.random.fold_in(seeds[11], 71), 0)
    values = scatter_about(seeds[4], (TOKENS, KVH * HD), 1.0, 6.0, ((0, 32),))
    lengths = draw_lengths(jax.random.fold_in(seeds[11], 71), 0)
    loss_counts = draw_loss_counts(jax.random.fold_in(seeds[11], 71), 0)
    query_weight = scatter_about(seeds[7], (D, H * HD), D ** -0.5, 0.0625, ((0, 32), (1, 16)))
    key_weight = scatter_about(seeds[8], (D, KVH * HD), D ** -0.5, 0.0625, ((0, 32), (1, 16)))
    value_weight = scatter_about(seeds[9], (D, KVH * HD), D ** -0.5, 0.0625, ((0, 32), (1, 16)))
    output_weight = scatter_about(seeds[10], (H * HD, D), (H * HD) ** -0.5, 0.09375, ((0, 16), (1, 32)))
    return {"inputs": inputs, "cotangent": cotangent, "queries": queries, "key_rows": key_rows, "values": values, "lengths": lengths, "loss_counts": loss_counts, "query_weight": query_weight, "key_weight": key_weight, "value_weight": value_weight, "output_weight": output_weight}


theta_base = 500000.0


def pack_positions(row_lengths, pack_rows):
    document_ends = jnp.cumsum(row_lengths).astype(jnp.int32)
    token_index = jnp.arange(pack_rows, dtype=jnp.int32)
    passed = token_index[:, None] >= document_ends[None, :]
    document_index = jnp.sum(passed.astype(jnp.int32), axis=1).astype(jnp.int32)
    offsets = jnp.sum(jnp.where(passed, row_lengths[None, :], 0), axis=1).astype(jnp.int32)
    return document_index, token_index - offsets


def rope_tables(positions, head_width):
    half_width = head_width // 2
    frequency = theta_base ** (-2.0 * jnp.arange(half_width, dtype=jnp.float32) / head_width)
    phases = positions.astype(jnp.float32)[:, None] * frequency[None, :]
    return jnp.cos(phases), jnp.sin(phases)


def rope_back(gradient, cosine, sine_table):
    half_width = gradient.shape[-1] // 2
    front_half = gradient[..., :half_width]
    back_half = gradient[..., half_width:]
    cos_rows = cosine[:, None, :]
    sin_rows = sine_table[:, None, :]
    return jnp.concatenate([front_half * cos_rows + back_half * sin_rows, back_half * cos_rows - front_half * sin_rows], axis=-1)


def reference(inputs, cotangent, queries, key_rows, values, lengths, loss_counts, query_weight, key_weight, value_weight, output_weight):
    token_total = inputs.shape[0]
    block_width = D // N_DP
    cot_blocks = cotangent.reshape(token_total, N_DP, block_width).transpose(1, 0, 2)
    out_blocks = output_weight.reshape(H * HD, N_DP, block_width).transpose(1, 0, 2)

    def add_out(running, block_pair):
        term_rows = jnp.dot(block_pair[0], block_pair[1].T, preferred_element_type=jnp.float32)
        return running + lax.optimization_barrier(term_rows.astype(jnp.bfloat16)).astype(jnp.float32), None

    out_sum, _ = lax.scan(add_out, jnp.zeros((token_total, H * HD), jnp.float32), (cot_blocks, out_blocks))
    grad_attended = out_sum.astype(jnp.bfloat16)
    group_width = H // KVH
    score_scale = HD ** -0.5

    def one_pack(pack_data):
        query_pack, key_pack, value_pack, grad_pack, row_lengths = pack_data
        pack_rows = query_pack.shape[0]
        document_index, positions = pack_positions(row_lengths, pack_rows)
        token_index = jnp.arange(pack_rows, dtype=jnp.int32)
        allowed = (document_index[:, None] == document_index[None, :]) & (token_index[None, :] <= token_index[:, None])
        query_four = query_pack.reshape(pack_rows, KVH, group_width, HD).astype(jnp.float32)
        key_three = key_pack.reshape(pack_rows, KVH, HD).astype(jnp.float32)
        value_three = value_pack.reshape(pack_rows, KVH, HD).astype(jnp.float32)
        grad_four = grad_pack.reshape(pack_rows, KVH, group_width, HD).astype(jnp.float32)
        scores = jnp.einsum('qkgd,skd->kgqs', query_four, key_three) * score_scale
        scores = jnp.where(allowed[None, None], scores, -jnp.inf)
        top_score = jnp.max(scores, axis=-1, keepdims=True)
        exponent = jnp.exp(scores - top_score)
        probs = exponent / jnp.sum(exponent, axis=-1, keepdims=True)
        probs_b = lax.optimization_barrier(probs.astype(jnp.bfloat16)).astype(jnp.float32)
        attended = jnp.einsum('kgqs,skd->qkgd', probs_b, value_three).astype(jnp.bfloat16)
        prob_grad = jnp.einsum('qkgd,skd->kgqs', grad_four, value_three)
        row_dot = jnp.sum(grad_four * attended.astype(jnp.float32), axis=-1).transpose(1, 2, 0)
        score_grad = probs * (prob_grad - row_dot[..., None])
        score_grad_b = lax.optimization_barrier(score_grad.astype(jnp.bfloat16)).astype(jnp.float32)
        query_post = jnp.einsum('kgqs,skd->qkgd', score_grad_b, key_three) * score_scale
        key_post = jnp.einsum('kgqs,qkgd->skd', score_grad_b, query_four) * score_scale
        value_post = jnp.einsum('kgqs,qkgd->skd', probs_b, grad_four)
        cosine, sine_table = rope_tables(positions, HD)
        query_grad = rope_back(query_post.reshape(pack_rows, H, HD), cosine, sine_table).astype(jnp.bfloat16)
        key_grad = rope_back(key_post, cosine, sine_table).astype(jnp.bfloat16)
        return query_grad, key_grad, value_post.astype(jnp.bfloat16), attended

    packed = (queries.reshape(N_DP, TOK_DEV, H * HD), key_rows.reshape(N_DP, TOK_DEV, KVH * HD),
              values.reshape(N_DP, TOK_DEV, KVH * HD), grad_attended.reshape(N_DP, TOK_DEV, H * HD), lengths)
    query_grad, key_grad, value_grad, attended = lax.map(one_pack, packed)
    query_grad = query_grad.reshape(token_total, H * HD)
    key_grad = key_grad.reshape(token_total, KVH * HD)
    value_grad = value_grad.reshape(token_total, KVH * HD)
    attended = attended.reshape(token_total, H * HD)
    inv_count = 1.0 / jnp.sum(loss_counts.astype(jnp.float32))
    query_gradient = (jnp.dot(inputs.T, query_grad, preferred_element_type=jnp.float32) * inv_count).astype(jnp.bfloat16)
    key_gradient = (jnp.dot(inputs.T, key_grad, preferred_element_type=jnp.float32) * inv_count).astype(jnp.bfloat16)
    value_gradient = (jnp.dot(inputs.T, value_grad, preferred_element_type=jnp.float32) * inv_count).astype(jnp.bfloat16)
    output_gradient = (jnp.dot(attended.T, cotangent, preferred_element_type=jnp.float32) * inv_count).astype(jnp.bfloat16)
    query_cols = H * HD // N_TENSOR
    kv_cols = KVH * HD // N_TENSOR

    def add_in(running, tensor_block):
        query_start = (tensor_block * query_cols).astype(jnp.int32)
        kv_start = (tensor_block * kv_cols).astype(jnp.int32)
        term_rows = jnp.dot(lax.dynamic_slice_in_dim(query_grad, query_start, query_cols, 1),
                            lax.dynamic_slice_in_dim(query_weight, query_start, query_cols, 1).T, preferred_element_type=jnp.float32)
        term_rows = term_rows + jnp.dot(lax.dynamic_slice_in_dim(key_grad, kv_start, kv_cols, 1),
                                        lax.dynamic_slice_in_dim(key_weight, kv_start, kv_cols, 1).T, preferred_element_type=jnp.float32)
        term_rows = term_rows + jnp.dot(lax.dynamic_slice_in_dim(value_grad, kv_start, kv_cols, 1),
                                        lax.dynamic_slice_in_dim(value_weight, kv_start, kv_cols, 1).T, preferred_element_type=jnp.float32)
        return running + lax.optimization_barrier(term_rows.astype(jnp.bfloat16)).astype(jnp.float32), None

    in_sum, _ = lax.scan(add_in, jnp.zeros((token_total, D), jnp.float32), jnp.arange(N_TENSOR, dtype=jnp.int32))
    input_gradient = (in_sum * inv_count).astype(jnp.bfloat16)
    return input_gradient, query_gradient, key_gradient, value_gradient, output_gradient
```

```python
import math

import jax
import jax.numpy as jnp
from jax import lax
from jax.experimental import pallas as pl
from jax.experimental.pallas import tpu as pltpu
from jax.sharding import PartitionSpec as P

NX, NY, NZ = 4, 8, 8
HD = 128
PACK = 128
DOCS = 8
BLOCK = 256
THETA = 500000.0
ORDER = (0, 1, 7, 2, 6, 3, 5, 4)
ATT_ROWS = 2 * HD + 16
PAY_ROWS = PACK + 32
F32 = jnp.float32
BF16 = jnp.bfloat16
NT = (((1,), (1,)), ((), ()))


def dot_nn(a, b):
    return jnp.dot(a, b, preferred_element_type=F32)


def dot_nt(a, b):
    return lax.dot_general(a, b, NT, preferred_element_type=F32)


def dot_tn(a, b):
    return dot_nn(a.astype(F32).T.astype(BF16), b)


def kernel(
    in_ref,
    cot_ref,
    q_ref,
    k_ref,
    v_ref,
    len_ref,
    cnt_ref,
    wq_ref,
    wk_ref,
    wv_ref,
    wo_ref,
    gin_ref,
    gq_ref,
    gk_ref,
    gv_ref,
    go_ref,
    cot_all,
    in_all,
    att_all,
    pay_all,
    b_right,
    b_left,
    keep_right,
    keep_left,
    keep_own,
    from_left,
    from_right,
    sum_right,
    sum_left,
    row_out,
    row_in,
    grad_own,
    probs_s,
    att_s,
    cos_s,
    sin_s,
    kv_out,
    kv_in,
    w_kv,
    q_acc,
    kv_acc,
    o_acc,
    term_own,
    sib_out,
    sib_in,
    chain_out,
    chain_in,
    fin,
    send_sems,
    recv_sems,
):
    d = lax.axis_index("dp")
    t = lax.axis_index("tensor")
    y, x = lax.div(d, NX), lax.rem(d, NX)
    z, c = lax.div(t, 2), lax.rem(t, 2)

    def at_z(zz, cc=c):
        return (d, lax.rem(zz, NZ) * 2 + cc)

    def at_x(xx):
        return (y * NX + lax.rem(xx, NX), t)

    def at_y(yy):
        return (lax.rem(yy, NY) * NX + x, t)

    sibling = (d, z * 2 + 1 - c)
    z_up, z_down = at_z(z + 1), at_z(z + NZ - 1)
    x_up, x_down = at_x(x + 1), at_x(x + NX - 1)
    y_up, y_down = at_y(y + 1), at_y(y + NY - 1)
    z_pair = z + 1 - 2 * lax.rem(z, 2)
    pair_same, pair_other = at_z(z_pair), at_z(z_pair, 1 - c)

    peers = [sibling, z_up, z_down, x_up, x_down, pair_other] + [at_y(y + j) for j in range(1, NY)]
    barrier = pltpu.get_barrier_semaphore()
    for peer in peers:
        pl.semaphore_signal(barrier, inc=1, device_id=peer, device_id_type=pl.DeviceIdType.MESH)
    pl.semaphore_wait(barrier, len(peers))

    used = [0]
    drain = []

    def new(count=1):
        used[0] += count
        return used[0] - count

    def copy_of(src, dst, dev, si, ri):
        return pltpu.make_async_remote_copy(
            src_ref=src,
            dst_ref=dst,
            send_sem=send_sems.at[si],
            recv_sem=recv_sems.at[ri],
            device_id=dev,
            device_id_type=pl.DeviceIdType.MESH,
        )

    def send(src, dst, dev, ri, si=None, when=None, like=None):
        copy = copy_of(src, dst, dev, ri if si is None else si, ri)
        copy.start()
        if when is None:
            drain.append((copy, None))
        else:
            drain.append(((like, si), when))

    def wait(dst, ri, dev=sibling):
        copy_of(dst, dst, dev, ri, ri).wait_recv()

    def z_gather(buf, rows):
        half = rows // 2
        up = {s: new() for s in range(1, 5)}
        down = {s: new() for s in range(1, 5)}
        sib = {o: new() for o in range(8)}

        def start():
            own = buf.at[0, c]
            send(own, buf.at[7, c], z_up, up[1])
            send(own, buf.at[1, c], z_down, down[1])
            send(own, buf.at[0, c], sibling, sib[0])

        def step(s):
            lo, hi = (8 - s) % 8, s
            if s < 4:
                for o, sems, dev, first in ((lo, up, z_up, 0), (hi, down, z_down, half)):
                    wait(buf.at[o, c], sems[s])
                    to = (o - 1) % 8 if dev is z_up else (o + 1) % 8
                    if s < 3:
                        send(buf.at[o, c], buf.at[to, c], dev, sems[s + 1])
                    else:
                        part = pl.ds(first, half)
                        send(buf.at[o, c, part], buf.at[to, c, part], dev, sems[4])
                    send(buf.at[o, c], buf.at[o, c], sibling, sib[o])
            else:
                wait(buf.at[4, c, pl.ds(0, half)], up[4])
                wait(buf.at[4, c, pl.ds(half, half)], down[4])
                send(buf.at[4, c], buf.at[4, c], sibling, sib[4])

        def wait_sibling(o):
            wait(buf.at[o, 1 - c], sib[o])

        return start, step, wait_sibling

    cot_all[0, c] = cot_ref[...]
    cot_start, cot_step, cot_sibling = z_gather(cot_all, BLOCK)
    in_start, in_step, in_sibling = z_gather(in_all, BLOCK)
    cot_start()

    rows_i = lax.broadcasted_iota(jnp.int32, (PACK, PACK), 0)
    cols_i = lax.broadcasted_iota(jnp.int32, (PACK, PACK), 1)
    end = 0
    doc_row = jnp.zeros((PACK, PACK), jnp.int32)
    doc_col = jnp.zeros((PACK, PACK), jnp.int32)
    first = jnp.zeros((PACK, PACK), jnp.int32)
    for j in range(DOCS):
        length = len_ref[0, j]
        end = end + length
        passed = rows_i >= end
        doc_row = doc_row + passed.astype(jnp.int32)
        doc_col = doc_col + (cols_i >= end).astype(jnp.int32)
        first = first + jnp.where(passed, length, 0)
    allowed = (doc_row == doc_col) & (cols_i <= rows_i)
    kv_head = pl.multiple_of(lax.div(t, 4) * HD, HD)
    scale = HD ** (-0.5)
    for h in range(2):
        scores = dot_nt(q_ref[:, h * HD : (h + 1) * HD], k_ref[:, pl.ds(kv_head, HD)]) * scale
        scores = jnp.where(allowed, scores, -jnp.inf)
        exponent = jnp.exp(scores - jnp.max(scores, axis=1, keepdims=True))
        probs = exponent / jnp.sum(exponent, axis=1, keepdims=True)
        probs_s[h] = probs
        attended = dot_nn(probs.astype(BF16), v_ref[:, pl.ds(kv_head, HD)]).astype(BF16)
        att_s[h] = attended.astype(F32)
        att_all[0, x, h * HD : (h + 1) * HD, :] = attended.astype(F32).T.astype(BF16)
    count = cnt_ref[0].astype(F32)
    att_all[0, x, 2 * HD : ATT_ROWS, :] = jnp.full((16, PACK), 1.0, F32).astype(BF16) * jnp.full((16, PACK), count, F32).astype(BF16)

    att_half = ATT_ROWS // 2
    ax_up, ax_down, ax_up2, ax_down2 = new(), new(), new(), new()
    send(att_all.at[0, x], att_all.at[0, x], x_up, ax_up)
    send(att_all.at[0, x], att_all.at[0, x], x_down, ax_down)
    x_m, x_p, x_2 = lax.rem(x + 3, NX), lax.rem(x + 1, NX), lax.rem(x + 2, NX)
    part_a, part_b = pl.ds(0, att_half), pl.ds(att_half, att_half)

    def att_x_forward():
        wait(att_all.at[0, x_m], ax_up)
        send(att_all.at[0, x_m, part_a], att_all.at[0, x_m, part_a], x_up, ax_up2)
        wait(att_all.at[0, x_p], ax_down)
        send(att_all.at[0, x_p, part_b], att_all.at[0, x_p, part_b], x_down, ax_down2)

    ay_up = {s: new() for s in range(1, 5)}
    ay_down = {s: new() for s in range(1, 5)}

    def att_y_start():
        wait(att_all.at[0, x_2, part_a], ax_up2)
        wait(att_all.at[0, x_2, part_b], ax_down2)
        send(att_all.at[0], att_all.at[7], y_up, ay_up[1])
        send(att_all.at[0], att_all.at[1], y_down, ay_down[1])

    def att_y_step(s):
        lo, hi = 8 - s, s
        if s < 4:
            wait(att_all.at[lo], ay_up[s])
            if s < 3:
                send(att_all.at[lo], att_all.at[lo - 1], y_up, ay_up[s + 1])
            else:
                send(att_all.at[lo, 0:2], att_all.at[lo - 1, 0:2], y_up, ay_up[4])
            wait(att_all.at[hi], ay_down[s])
            if s < 3:
                send(att_all.at[hi], att_all.at[hi + 1], y_down, ay_down[s + 1])
            else:
                send(att_all.at[hi, 2:4], att_all.at[hi + 1, 2:4], y_down, ay_down[4])
        else:
            wait(att_all.at[4, 0:2], ay_up[4])
            wait(att_all.at[4, 2:4], ay_down[4])

    lane = jnp.where(cols_i < HD // 2, cols_i, cols_i - HD // 2)
    frequency = jnp.exp(lane.astype(F32) * (-2.0 * math.log(THETA) / HD))
    phases = (rows_i - first).astype(F32) * frequency
    cos_s[...] = jnp.cos(phases)
    sines = jnp.sin(phases)
    sin_s[...] = jnp.where(cols_i < HD // 2, sines, -sines)
    in_all[0, c] = in_ref[...].astype(F32).T.astype(BF16)
    place_r = lax.broadcasted_iota(jnp.int32, (32, HD), 0)
    place_c = lax.broadcasted_iota(jnp.int32, (32, HD), 1)
    w_kv[...] = (
        dot_nn(wk_ref[...], (place_r == place_c).astype(BF16))
        + dot_nn(wv_ref[...], (place_r + 32 == place_c).astype(BF16))
    ).astype(BF16)
    q_acc[...] = jnp.zeros_like(q_acc)
    kv_acc[...] = jnp.zeros_like(kv_acc)
    o_acc[...] = jnp.zeros_like(o_acc)

    bx_up, bx_down, bx_up2, bx_down2 = new(8), new(8), new(8), new(8)
    by_send, by_recv = new(8), new(8)

    def b_terms(i):
        o = ORDER[i]

        def term(r):
            xx = lax.rem(x + r, NX)
            start = pl.multiple_of(lax.rem(xx, 2) * PACK, PACK)
            return dot_nt(cot_all[o, lax.div(xx, 2), pl.ds(start, PACK), :], wo_ref[...])

        far = term(2).astype(BF16)
        b_right[i, 0:64] = far[64:]
        b_left[i, 0:64] = far[:64]
        right = term(1)
        b_right[i, 64:128] = right[:64].astype(BF16)
        send(b_right.at[i], from_left.at[i, 0:128], x_up, bx_up + i)
        left = term(3)
        b_left[i, 64:128] = left[64:].astype(BF16)
        send(b_left.at[i], from_right.at[i, 0:128], x_down, bx_down + i)
        keep_right[i] = right[64:]
        keep_left[i] = left[:64]
        keep_own[i] = term(0)

    def b_forward(i):
        wait(from_left.at[i, 0:128], bx_up + i)
        sum_right[i] = (keep_right[i] + from_left[i, 0:64].astype(F32)).astype(BF16)
        send(sum_right.at[i], from_left.at[i, 128:192], x_up, bx_up2 + i)
        wait(from_right.at[i, 0:128], bx_down + i)
        sum_left[i] = (keep_left[i] + from_right[i, 0:64].astype(F32)).astype(BF16)
        send(sum_left.at[i], from_right.at[i, 128:192], x_down, bx_down2 + i)

    def b_finish(i):
        wait(from_left.at[i, 128:192], bx_up2 + i)
        wait(from_right.at[i, 128:192], bx_down2 + i)
        top = keep_own[i, 0:64] + from_left[i, 64:128].astype(F32) + from_right[i, 128:192].astype(F32)
        low = keep_own[i, 64:128] + from_left[i, 128:192].astype(F32) + from_right[i, 64:128].astype(F32)
        row = lax.rem(z + ORDER[i], NY)
        hops = lax.rem(row - y + NY, NY)

        @pl.when(hops == 0)
        def _():
            grad_own[0:64] = top
            grad_own[64:128] = low

        away = hops != 0

        @pl.when(away)
        def _():
            row_out[i, 0:64] = top.astype(BF16)
            row_out[i, 64:128] = low.astype(BF16)
            send(row_out.at[i], row_in.at[hops], at_y(row), by_recv + hops, by_send + i, away, (row_in, i))

    for i in range(10):
        if i < 8:
            if i in (1, 3, 5):
                cot_step((i + 1) // 2)
            if i == 7:
                cot_step(4)
                in_start()
            cot_sibling(ORDER[i])
            b_terms(i)
        if 1 <= i < 9:
            b_forward(i - 1)
        if i >= 2:
            b_finish(i - 2)
        if i == 1:
            att_x_forward()
        if i == 3:
            att_y_start()
    in_step(1)
    att_y_step(1)

    grad = grad_own[...]
    for j in range(1, NY):
        wait(row_in.at[j], by_recv + j)
        grad = grad + row_in[j].astype(F32)
    grad_b = grad.astype(BF16)

    def rotate_back(value):
        return value * cos_s[...] + pltpu.roll(value, HD // 2, 1) * sin_s[...]

    key_post = jnp.zeros((PACK, HD), F32)
    value_post = jnp.zeros((PACK, HD), F32)
    for h in range(2):
        grad_h = grad_b[:, h * HD : (h + 1) * HD]
        query_h = q_ref[:, h * HD : (h + 1) * HD]
        probs = probs_s[h]
        prob_grad = dot_nt(grad_h, v_ref[:, pl.ds(kv_head, HD)])
        row_dot = jnp.sum(grad_h.astype(F32) * att_s[h], axis=1, keepdims=True)
        score_grad = (probs * (prob_grad - row_dot)).astype(BF16)
        query_post = dot_nn(score_grad, k_ref[:, pl.ds(kv_head, HD)]) * scale
        pay_all[0, x, 0:PACK, h * HD : (h + 1) * HD] = rotate_back(query_post).astype(BF16)
        key_post = key_post + dot_tn(score_grad, query_h) * scale
        value_post = value_post + dot_tn(probs.astype(BF16), grad_h)
    key_sum = rotate_back(key_post).astype(BF16)
    value_sum = value_post.astype(BF16)
    sel_r = lax.broadcasted_iota(jnp.int32, (HD, BLOCK), 0)
    sel_c = lax.broadcasted_iota(jnp.int32, (HD, BLOCK), 1)
    key_to = sel_r + 32 * ((sel_r >= 32).astype(jnp.int32) + (sel_r >= 64).astype(jnp.int32) + (sel_r >= 96).astype(jnp.int32))
    packed = dot_nn(key_sum, (sel_c == key_to).astype(BF16)) + dot_nn(
        value_sum, (sel_c == key_to + 32).astype(BF16)
    )
    kv_out[0] = packed[:, :HD].astype(BF16)
    kv_out[1] = packed[:, HD:].astype(BF16)
    kv_sem = new(4)
    half_own = lax.rem(z, 2)
    send(kv_out.at[half_own], kv_in.at[1], sibling, kv_sem + 1)
    send(kv_out.at[1 - half_own], kv_in.at[2], pair_same, kv_sem + 2)
    send(kv_out.at[1 - half_own], kv_in.at[3], pair_other, kv_sem + 3)
    in_step(2)
    att_y_step(2)
    kv_total = kv_out[half_own].astype(F32)
    for j in range(1, 4):
        wait(kv_in.at[j], kv_sem + j)
        kv_total = kv_total + kv_in[j].astype(F32)
    kv_total = jnp.where(c == 1, pltpu.roll(kv_total, HD // 2, 1), kv_total)
    low_lane = lax.broadcasted_iota(jnp.int32, (32, HD), 1) < HD // 2
    for j in range(2):
        part = jnp.where(
            low_lane,
            kv_total[64 * j : 64 * j + 32],
            pltpu.roll(kv_total[64 * j + 32 : 64 * j + 64], HD // 2, 1),
        )
        pay_all[0, x, PACK:PAY_ROWS, j * HD : (j + 1) * HD] = part.astype(BF16)

    pay_half = PAY_ROWS // 2
    head, tail = pl.ds(0, pay_half), pl.ds(pay_half, pay_half)
    dy_up = {s: new() for s in range(1, 5)}
    dy_down = {s: new() for s in range(1, 5)}
    dx_up, dx_down, dx_up2, dx_down2 = new(8), new(8), new(8), new(8)

    def d_receive(i):
        o = ORDER[i]
        mine = pay_all.at[o, x]
        if o == 0:
            send(mine, pay_all.at[7, x], y_up, dy_up[1])
            send(mine, pay_all.at[1, x], y_down, dy_down[1])
        elif o == 4:
            wait(pay_all.at[4, x, head], dy_up[4])
            wait(pay_all.at[4, x, tail], dy_down[4])
        elif o < 4:
            wait(mine, dy_down[o])
            if o < 3:
                send(mine, pay_all.at[o + 1, x], y_down, dy_down[o + 1])
            else:
                send(pay_all.at[o, x, tail], pay_all.at[4, x, tail], y_down, dy_down[4])
        else:
            s = 8 - o
            wait(mine, dy_up[s])
            if s < 3:
                send(mine, pay_all.at[o - 1, x], y_up, dy_up[s + 1])
            else:
                send(pay_all.at[o, x, head], pay_all.at[4, x, head], y_up, dy_up[4])
        send(mine, mine, x_up, dx_up + i)
        send(mine, mine, x_down, dx_down + i)

    def d_forward(i):
        o = ORDER[i]
        wait(pay_all.at[o, x_m], dx_up + i)
        send(pay_all.at[o, x_m, head], pay_all.at[o, x_m, head], x_up, dx_up2 + i)
        wait(pay_all.at[o, x_p], dx_down + i)
        send(pay_all.at[o, x_p, tail], pay_all.at[o, x_p, tail], x_down, dx_down2 + i)

    sib_sem = new(8)

    def unpack(o, xx):
        raw = pay_all[o, xx, PACK:PAY_ROWS, :].astype(F32)
        parts = []
        for j in range(2):
            part = raw[:, j * HD : (j + 1) * HD]
            parts += [part, pltpu.roll(part, HD // 2, 1)]
        return jnp.concatenate(parts, axis=0).astype(BF16)

    def d_compute(i):
        o = ORDER[i]
        wait(pay_all.at[o, x_2, head], dx_up2 + i)
        wait(pay_all.at[o, x_2, tail], dx_down2 + i)
        oz = lax.rem(y + o - z + NZ, NZ)
        for own in (False, True):
            cc = c if own else 1 - c
            query = jnp.concatenate(
                [pay_all[o, 2 * cc, 0:PACK, :], pay_all[o, 2 * cc + 1, 0:PACK, :]], axis=0
            )
            kv = jnp.concatenate([unpack(o, 2 * cc), unpack(o, 2 * cc + 1)], axis=0)
            rows = dot_nt(query, wq_ref[...]) + dot_nt(kv, w_kv[...])
            if own:
                term_own[i] = rows
            else:
                sib_out[i] = rows.astype(BF16)
                send(sib_out.at[i], sib_in.at[i], sibling, sib_sem + i)
            acts = in_all[oz, cc]
            q_acc[...] += dot_nn(acts, query)
            kv_acc[...] += dot_nn(acts, kv)

    chain_send = new(16)
    chain_recv = new(32)

    def chain_sem(i, side, half):
        return chain_recv + 4 * i + 2 * side + half

    def chain_add(i, half):
        part = pl.ds(half * PACK, PACK)
        return part, term_own[i, part, :]

    def f_sibling(i):
        wait(sib_in.at[i], sib_sem + i)
        term_own[i] = term_own[i] + sib_in[i].astype(F32)

    def f_hop(i, far):
        hops = lax.rem(y + ORDER[i] - z + NZ, NZ)
        if far == 4:
            here = hops == 4

            @pl.when(here)
            def _():
                chain_out[i] = term_own[i].astype(BF16)
                for half, dev in ((0, z_up), (1, z_down)):
                    part = pl.ds(half * PACK, PACK)
                    send(
                        chain_out.at[i, part],
                        chain_in.at[i, half, part],
                        dev,
                        chain_sem(i, half, half),
                        chain_send + 2 * i + half,
                        here,
                        (chain_out, i),
                    )

        elif far > 0:
            here = (hops == far) | (hops == NZ - far)
            side = (hops > 4).astype(jnp.int32)
            dev = at_z(z + 1 + side * (NZ - 2))

            @pl.when(here)
            def _():
                for step in range(2):
                    half = side if step == 0 else 1 - side
                    start = pl.multiple_of(half * PACK, PACK)
                    part = pl.ds(start, PACK)
                    total = term_own[i, part, :]
                    if far < 3 or step == 0:
                        wait(chain_in.at[i, side, part], chain_sem(i, side, half))
                        total = total + chain_in[i, side, part, :].astype(F32)
                    chain_out[i, part, :] = total.astype(BF16)
                    send(
                        chain_out.at[i, part],
                        chain_in.at[i, side, part],
                        dev,
                        chain_sem(i, side, half),
                        chain_send + 2 * i + step,
                        here,
                        (chain_out, i),
                    )

        else:

            @pl.when(hops == 0)
            def _():
                for half in range(2):
                    part = pl.ds(half * PACK, PACK)
                    total = term_own[i, part, :]
                    for side in range(2):
                        wait(chain_in.at[i, side, part], chain_sem(i, side, half))
                        total = total + chain_in[i, side, part, :].astype(F32)
                    fin[part, :] = total

    def o_compute(o):
        oz = lax.rem(y + o - z + NZ, NZ)
        total = o_acc[...]
        for xx in range(NX):
            sub = (xx % 2) * PACK
            total = total + dot_nn(att_all[o, xx, 0 : 2 * HD, :], cot_all[oz, xx // 2, sub : sub + PACK, :])
        o_acc[...] = total

    for i in range(16):
        if i < 8:
            d_receive(i)
        if i == 1:
            in_step(3)
        if i == 2:
            in_step(4)
            for o in range(8):
                in_sibling(o)
        if 1 <= i < 9:
            d_forward(i - 1)
        if 2 <= i < 10:
            d_compute(i - 2)
        if 3 <= i < 11:
            f_sibling(i - 3)
        for far in (4, 3, 2, 1, 0):
            if 0 <= i - 3 - (4 - far) < 8:
                f_hop(i - 3 - (4 - far), far)
        if i == 3:
            att_y_step(3)
            for o in (0, 1, 7):
                o_compute(o)
        if i == 5:
            for o in (2, 6):
                o_compute(o)
        if i == 7:
            att_y_step(4)
            for o in (3, 5, 4):
                o_compute(o)

    total = jnp.zeros((16, PACK), F32)
    for o in range(8):
        for xx in range(NX):
            total = total + att_all[o, xx, 2 * HD : ATT_ROWS, :].astype(F32)
    inv = 1.0 / total[0:1, 0:1]
    gin_ref[...] = (fin[...] * inv).astype(BF16)
    gq_ref[...] = (q_acc[...] * inv).astype(BF16)
    kv_sum = kv_acc[...] * inv
    gk_ref[...] = kv_sum[:, 0:32].astype(BF16)
    gv_ref[...] = pltpu.roll(kv_sum, HD - 32, 1)[:, 0:32].astype(BF16)
    go_ref[...] = (o_acc[...] * inv).astype(BF16)

    for copy, when in drain:
        if when is None:
            copy.wait_send()
        else:
            (buf, i), sem = copy

            @pl.when(when)
            def _():
                like = buf.at[i, 0:PACK]
                copy_of(like, like, sibling, sem, sem).wait_send()

    assert used[0] <= SEMS, used[0]


SEMS = 256


def on_device(*args):
    vmem = pl.BlockSpec(memory_space=pltpu.VMEM)
    smem = pl.BlockSpec(memory_space=pltpu.SMEM)
    sd = jax.ShapeDtypeStruct
    return pl.pallas_call(
        kernel,
        out_shape=(
            sd((BLOCK, BLOCK), BF16),
            sd((BLOCK, BLOCK), BF16),
            sd((BLOCK, 32), BF16),
            sd((BLOCK, 32), BF16),
            sd((BLOCK, BLOCK), BF16),
        ),
        in_specs=[vmem] * 5 + [smem] * 2 + [vmem] * 4,
        out_specs=(vmem,) * 5,
        scratch_shapes=[
            pltpu.VMEM((8, 2, BLOCK, BLOCK), BF16),
            pltpu.VMEM((8, 2, BLOCK, BLOCK), BF16),
            pltpu.VMEM((8, NX, ATT_ROWS, PACK), BF16),
            pltpu.VMEM((8, NX, PAY_ROWS, BLOCK), BF16),
            pltpu.VMEM((8, PACK, BLOCK), BF16),
            pltpu.VMEM((8, PACK, BLOCK), BF16),
            pltpu.VMEM((8, 64, BLOCK), F32),
            pltpu.VMEM((8, 64, BLOCK), F32),
            pltpu.VMEM((8, PACK, BLOCK), F32),
            pltpu.VMEM((8, 192, BLOCK), BF16),
            pltpu.VMEM((8, 192, BLOCK), BF16),
            pltpu.VMEM((8, 64, BLOCK), BF16),
            pltpu.VMEM((8, 64, BLOCK), BF16),
            pltpu.VMEM((8, PACK, BLOCK), BF16),
            pltpu.VMEM((8, PACK, BLOCK), BF16),
            pltpu.VMEM((PACK, BLOCK), F32),
            pltpu.VMEM((2, PACK, PACK), F32),
            pltpu.VMEM((2, PACK, HD), F32),
            pltpu.VMEM((PACK, HD), F32),
            pltpu.VMEM((PACK, HD), F32),
            pltpu.VMEM((2, PACK, HD), BF16),
            pltpu.VMEM((4, PACK, HD), BF16),
            pltpu.VMEM((BLOCK, HD), BF16),
            pltpu.VMEM((BLOCK, BLOCK), F32),
            pltpu.VMEM((BLOCK, HD), F32),
            pltpu.VMEM((BLOCK, BLOCK), F32),
            pltpu.VMEM((8, BLOCK, BLOCK), F32),
            pltpu.VMEM((8, BLOCK, BLOCK), BF16),
            pltpu.VMEM((8, BLOCK, BLOCK), BF16),
            pltpu.VMEM((8, BLOCK, BLOCK), BF16),
            pltpu.VMEM((8, 2, BLOCK, BLOCK), BF16),
            pltpu.VMEM((BLOCK, BLOCK), F32),
            pltpu.SemaphoreType.DMA((SEMS,)),
            pltpu.SemaphoreType.DMA((SEMS,)),
        ],
        compiler_params=pltpu.CompilerParams(
            collective_id=0, has_side_effects=True, vmem_limit_bytes=50 * 1024 * 1024
        ),
        name="attention_block_backward",
    )(*args)


def solution(mesh):
    return jax.shard_map(
        on_device,
        mesh=mesh,
        in_specs=(
            P("tensor", "dp"),
            P("tensor", "dp"),
            P("dp", "tensor"),
            P("dp", None),
            P("dp", None),
            P("dp", None),
            P("dp"),
            P("dp", "tensor"),
            P("dp", "tensor"),
            P("dp", "tensor"),
            P("tensor", "dp"),
        ),
        out_specs=(
            P("tensor", "dp"),
            P("dp", "tensor"),
            P("dp", "tensor"),
            P("dp", "tensor"),
            P("tensor", "dp"),
        ),
        check_vma=False,
    )
```

```python
import math

import jax
import jax.numpy as jnp
from jax import lax
from jax.experimental import pallas as pl
from jax.experimental.pallas import tpu as pltpu
from jax.sharding import PartitionSpec as P

NX, NY, NZ = 4, 8, 8
HD = 128
PACK = 128
DOCS = 8
BLOCK = 256
THETA = 500000.0
ORDER = (0, 1, 7, 2, 6, 3, 5, 4)
ATT_ROWS = 2 * HD + 16
DIRECT = 7
F32 = jnp.float32
BF16 = jnp.bfloat16
NT = (((1,), (1,)), ((), ()))


def dot_nn(a, b):
    return jnp.dot(a, b, preferred_element_type=F32)


def dot_nt(a, b):
    return lax.dot_general(a, b, NT, preferred_element_type=F32)


def dot_tn(a, b):
    return dot_nn(a.astype(F32).T.astype(BF16), b)


def kernel(
    in_ref,
    cot_ref,
    q_ref,
    k_ref,
    v_ref,
    len_ref,
    cnt_ref,
    wq_ref,
    wk_ref,
    wv_ref,
    wo_ref,
    gin_ref,
    gq_ref,
    gk_ref,
    gv_ref,
    go_ref,
    cot_all,
    in_all,
    att_all,
    q_all,
    kv_all,
    kv_rows,
    x_out,
    x_in,
    b_right,
    b_left,
    keep_right,
    keep_left,
    keep_own,
    from_left,
    from_right,
    sum_right,
    sum_left,
    row_out,
    row_in,
    grad_own,
    probs_s,
    att_s,
    cos_s,
    sin_s,
    kv_out,
    kv_in,
    w_kv,
    q_acc,
    kv_acc,
    o_acc,
    term_own,
    sib_out,
    sib_in,
    chain_out,
    chain_in,
    fin,
    in_raw,
    q_s,
    k_s,
    v_s,
    wq_s,
    wo_s,
    len_s,
    cnt_s,
    send_sems,
    recv_sems,
    load_sems,
):
    d = lax.axis_index("dp")
    t = lax.axis_index("tensor")
    y, x = lax.div(d, NX), lax.rem(d, NX)
    z, c = lax.div(t, 2), lax.rem(t, 2)

    def at_z(zz, cc=c):
        return (d, lax.rem(zz, NZ) * 2 + cc)

    def at_x(xx):
        return (y * NX + lax.rem(xx, NX), t)

    def at_y(yy):
        return (lax.rem(yy, NY) * NX + x, t)

    sibling = (d, z * 2 + 1 - c)
    z_up, z_down = at_z(z + 1), at_z(z + NZ - 1)
    x_up, x_down = at_x(x + 1), at_x(x + NX - 1)
    y_up, y_down = at_y(y + 1), at_y(y + NY - 1)
    z_pair = z + 1 - 2 * lax.rem(z, 2)
    pair_same, pair_other = at_z(z_pair), at_z(z_pair, 1 - c)

    kv_head = pl.multiple_of(lax.div(t, 4) * HD, HD)
    head_cols = pl.ds(kv_head, HD)
    loads = [
        pltpu.make_async_copy(src, dst, load_sems.at[i])
        for i, (src, dst) in enumerate(
            (
                (cot_ref, cot_all.at[0, c]),
                (len_ref, len_s),
                (cnt_ref, cnt_s),
                (q_ref, q_s),
                (k_ref.at[:, head_cols], k_s),
                (v_ref.at[:, head_cols], v_s),
                (wo_ref, wo_s),
                (in_ref, in_raw),
                (wk_ref, w_kv.at[0:32]),
                (wv_ref, w_kv.at[32:64]),
                (wq_ref, wq_s),
            )
        )
    ]
    for load in loads:
        load.start()

    peers = [sibling, pair_other]
    peers += [at_x(x + j) for j in range(1, NX)]
    peers += [at_y(y + j) for j in range(1, NY)]
    peers += [at_z(z + j) for j in (1, 2, 6, 7)]
    barrier = pltpu.get_barrier_semaphore()
    for peer in peers:
        pl.semaphore_signal(barrier, inc=1, device_id=peer, device_id_type=pl.DeviceIdType.MESH)
    pl.semaphore_wait(barrier, len(peers))

    used = [0]
    drain = []

    def new(count=1):
        used[0] += count
        return used[0] - count

    def copy_of(src, dst, dev, si, ri):
        return pltpu.make_async_remote_copy(
            src_ref=src,
            dst_ref=dst,
            send_sem=send_sems.at[si],
            recv_sem=recv_sems.at[ri],
            device_id=dev,
            device_id_type=pl.DeviceIdType.MESH,
        )

    def send(src, dst, dev, ri, si=None, when=None, like=None):
        copy = copy_of(src, dst, dev, ri if si is None else si, ri)
        copy.start()
        if when is None:
            drain.append((copy, None))
        else:
            drain.append(((like, si), when))

    def wait(dst, ri, dev=sibling):
        copy_of(dst, dst, dev, ri, ri).wait_recv()

    def z_gather(buf, rows):
        size = rows // 2
        part = [pl.ds(0, size), pl.ds(size, size)]
        up = {s: (new(), new()) for s in range(1, 5)}
        down = {s: (new(), new()) for s in range(1, 5)}
        sib = {o: (new(), new()) for o in range(8)}

        def start():
            for k in range(2):
                own = buf.at[0, c, part[k]]
                send(own, buf.at[7, c, part[k]], z_up, up[1][k])
                send(own, buf.at[1, c, part[k]], z_down, down[1][k])
            for k in range(2):
                own = buf.at[0, c, part[k]]
                send(own, own, sibling, sib[0][k])

        def step(s):
            lo, hi = (8 - s) % 8, s
            if s == 4:
                for k, sems in ((0, up), (1, down)):
                    here = buf.at[4, c, part[k]]
                    wait(here, sems[4][k])
                    send(here, here, sibling, sib[4][k])
                return
            order = ((lo, 0), (hi, 1), (lo, 1), (hi, 0)) if s == 3 else ((lo, 0), (hi, 0), (lo, 1), (hi, 1))
            for o, k in order:
                sems, dev, to = (up, z_up, o - 1) if o == lo else (down, z_down, o + 1)
                here = buf.at[o, c, part[k]]
                wait(here, sems[s][k])
                if s < 3 or k == (0 if o == lo else 1):
                    send(here, buf.at[to, c, part[k]], dev, sems[s + 1][k])
                send(here, here, sibling, sib[o][k])

        def wait_sibling(o):
            for k in range(2):
                wait(buf.at[o, 1 - c, part[k]], sib[o][k])

        return start, step, wait_sibling

    loads[0].wait()
    cot_start, cot_step, cot_sibling = z_gather(cot_all, BLOCK)
    in_start, in_step, in_sibling = z_gather(in_all, BLOCK)
    cot_start()

    for load in loads[1:6]:
        load.wait()
    rows_i = lax.broadcasted_iota(jnp.int32, (PACK, PACK), 0)
    cols_i = lax.broadcasted_iota(jnp.int32, (PACK, PACK), 1)
    end = 0
    doc_row = jnp.zeros((PACK, PACK), jnp.int32)
    doc_col = jnp.zeros((PACK, PACK), jnp.int32)
    first = jnp.zeros((PACK, PACK), jnp.int32)
    for j in range(DOCS):
        length = len_s[0, j]
        end = end + length
        passed = rows_i >= end
        doc_row = doc_row + passed.astype(jnp.int32)
        doc_col = doc_col + (cols_i >= end).astype(jnp.int32)
        first = first + jnp.where(passed, length, 0)
    allowed = (doc_row == doc_col) & (cols_i <= rows_i)
    scale = HD ** (-0.5)
    for h in range(2):
        scores = dot_nt(q_s[:, h * HD : (h + 1) * HD], k_s[...]) * scale
        scores = jnp.where(allowed, scores, -jnp.inf)
        exponent = jnp.exp(scores - jnp.max(scores, axis=1, keepdims=True))
        probs = exponent / jnp.sum(exponent, axis=1, keepdims=True)
        probs_s[h] = probs
        attended = dot_nn(probs.astype(BF16), v_s[...]).astype(BF16)
        att_s[h] = attended.astype(F32)
        att_all[0, x, h * HD : (h + 1) * HD, :] = attended.astype(F32).T.astype(BF16)
    count = cnt_s[0, 0].astype(F32)
    att_all[0, x, 2 * HD : ATT_ROWS, :] = jnp.full((16, PACK), 1.0, F32).astype(BF16) * jnp.full((16, PACK), count, F32).astype(BF16)

    ax = new(NX)
    for j in (1, 3, 2):
        send(att_all.at[0, x], att_all.at[0, x], at_x(x + j), ax + j)
    x_m, x_p, x_2 = lax.rem(x + 3, NX), lax.rem(x + 1, NX), lax.rem(x + 2, NX)

    def y_gather(buf):
        up = {s: new() for s in range(1, 5)}
        down = {s: new() for s in range(1, 5)}

        def start():
            send(buf.at[0], buf.at[7], y_up, up[1])
            send(buf.at[0], buf.at[1], y_down, down[1])

        def step(s):
            lo, hi = 8 - s, s
            if s == 4:
                wait(buf.at[4, 0:2], up[4])
                wait(buf.at[4, 2:4], down[4])
                return
            wait(buf.at[lo], up[s])
            if s < 3:
                send(buf.at[lo], buf.at[lo - 1], y_up, up[s + 1])
            else:
                send(buf.at[lo, 0:2], buf.at[lo - 1, 0:2], y_up, up[4])
            wait(buf.at[hi], down[s])
            if s < 3:
                send(buf.at[hi], buf.at[hi + 1], y_down, down[s + 1])
            else:
                send(buf.at[hi, 2:4], buf.at[hi + 1, 2:4], y_down, down[4])

        return start, step

    att_start, att_y_step = y_gather(att_all)
    kv_start, kv_y_step = y_gather(kv_all)

    def att_y_start():
        for j in range(1, NX):
            wait(att_all.at[0, lax.rem(x + NX - j, NX)], ax + j)
        att_start()

    def tables():
        lane = jnp.where(cols_i < HD // 2, cols_i, cols_i - HD // 2)
        frequency = jnp.exp(lane.astype(F32) * (-2.0 * math.log(THETA) / HD))
        phases = (rows_i - first).astype(F32) * frequency
        cos_s[...] = jnp.cos(phases)
        sines = jnp.sin(phases)
        sin_s[...] = jnp.where(cols_i < HD // 2, sines, -sines)
        for load in loads[7:]:
            load.wait()
        in_all[0, c] = in_raw[...].astype(F32).T.astype(BF16)
        w_kv[64:128] = jnp.zeros((64, BLOCK), BF16)
        q_acc[...] = jnp.zeros_like(q_acc)
        kv_acc[...] = jnp.zeros_like(kv_acc)
        o_acc[...] = jnp.zeros_like(o_acc)

    bx_up, bx_down, bx_up2, bx_down2 = new(8), new(8), new(8), new(8)
    bx_far = new(8)
    by_send, by_recv = new(8), new(8)

    def b_terms(i):
        o = ORDER[i]

        def term(r):
            xx = lax.rem(x + r, NX)
            start = pl.multiple_of(lax.rem(xx, 2) * PACK, PACK)
            return dot_nt(cot_all[o, lax.div(xx, 2), pl.ds(start, PACK), :], wo_s[...])

        if i >= DIRECT:
            for r, buf, sem in ((2, x_out, bx_far), (1, b_right, bx_up), (3, b_left, bx_down)):
                buf[i] = term(r).astype(BF16)
                send(buf.at[i], x_in.at[i, r], at_x(x + r), sem + i)
            keep_own[i] = term(0)
            return
        far = term(2).astype(BF16)
        b_right[i, 0:64] = far[64:]
        b_left[i, 0:64] = far[:64]
        right = term(1)
        b_right[i, 64:128] = right[:64].astype(BF16)
        send(b_right.at[i], from_left.at[i, 0:128], x_up, bx_up + i)
        left = term(3)
        b_left[i, 64:128] = left[64:].astype(BF16)
        send(b_left.at[i], from_right.at[i, 0:128], x_down, bx_down + i)
        keep_right[i] = right[64:]
        keep_left[i] = left[:64]
        keep_own[i] = term(0)

    def b_forward(i):
        wait(from_left.at[i, 0:128], bx_up + i)
        sum_right[i] = (keep_right[i] + from_left[i, 0:64].astype(F32)).astype(BF16)
        send(sum_right.at[i], from_left.at[i, 128:192], x_up, bx_up2 + i)
        wait(from_right.at[i, 0:128], bx_down + i)
        sum_left[i] = (keep_left[i] + from_right[i, 0:64].astype(F32)).astype(BF16)
        send(sum_left.at[i], from_right.at[i, 128:192], x_down, bx_down2 + i)

    def b_finish(i):
        if i >= DIRECT:
            whole = keep_own[i]
            for r, sem in ((1, bx_up), (3, bx_down), (2, bx_far)):
                wait(x_in.at[i, r], sem + i)
                whole = whole + x_in[i, r].astype(F32)
            top, low = whole[0:64], whole[64:128]
        else:
            top, low = b_ring_sum(i)
        row = lax.rem(z + ORDER[i], NY)
        hops = lax.rem(row - y + NY, NY)

        @pl.when(hops == 0)
        def _():
            grad_own[0:64] = top
            grad_own[64:128] = low

        away = hops != 0

        @pl.when(away)
        def _():
            row_out[i, 0:64] = top.astype(BF16)
            row_out[i, 64:128] = low.astype(BF16)
            send(row_out.at[i], row_in.at[hops], at_y(row), by_recv + hops, by_send + i, away, (row_in, i))

    def b_ring_sum(i):
        wait(from_left.at[i, 128:192], bx_up2 + i)
        wait(from_right.at[i, 128:192], bx_down2 + i)
        top = keep_own[i, 0:64] + from_left[i, 64:128].astype(F32) + from_right[i, 128:192].astype(F32)
        low = keep_own[i, 64:128] + from_left[i, 128:192].astype(F32) + from_right[i, 64:128].astype(F32)
        return top, low

    def rows_in(*steps):
        for i in steps:
            cot_sibling(ORDER[i])
            b_terms(i)

    kv_sem, kvx = new(4), new(NX)
    half_own = lax.rem(z, 2)

    def rotate_back(value):
        return value * cos_s[...] + pltpu.roll(value, HD // 2, 1) * sin_s[...]

    def backward():
        grad = grad_own[...]
        for j in range(1, NY):
            wait(row_in.at[j], by_recv + j)
            grad = grad + row_in[j].astype(F32)
        grad_b = grad.astype(BF16)
        key_post = jnp.zeros((PACK, HD), F32)
        value_post = jnp.zeros((PACK, HD), F32)
        for h in range(2):
            grad_h = grad_b[:, h * HD : (h + 1) * HD]
            probs = probs_s[h]
            prob_grad = dot_nt(grad_h, v_s[...])
            row_dot = jnp.sum(grad_h.astype(F32) * att_s[h], axis=1, keepdims=True)
            score_grad = (probs * (prob_grad - row_dot)).astype(BF16)
            query_post = dot_nn(score_grad, k_s[...]) * scale
            q_all[0, x, :, h * HD : (h + 1) * HD] = rotate_back(query_post).astype(BF16)
            key_post = key_post + dot_tn(score_grad, q_s[:, h * HD : (h + 1) * HD]) * scale
            value_post = value_post + dot_tn(probs.astype(BF16), grad_h)
        d_receive(0)
        key_sum = rotate_back(key_post).astype(BF16)
        value_sum = value_post.astype(BF16)
        sel_r = lax.broadcasted_iota(jnp.int32, (HD, BLOCK), 0)
        sel_c = lax.broadcasted_iota(jnp.int32, (HD, BLOCK), 1)
        key_to = sel_r
        for edge in (32, 64, 96):
            key_to = key_to + 32 * (sel_r >= edge).astype(jnp.int32)
        packed = dot_nn(key_sum, (sel_c == key_to).astype(BF16)) + dot_nn(
            value_sum, (sel_c == key_to + 32).astype(BF16)
        )
        kv_out[0] = packed[:, :HD].astype(BF16)
        kv_out[1] = packed[:, HD:].astype(BF16)
        send(kv_out.at[half_own], kv_in.at[1], sibling, kv_sem + 1)
        send(kv_out.at[1 - half_own], kv_in.at[2], pair_same, kv_sem + 2)
        send(kv_out.at[1 - half_own], kv_in.at[3], pair_other, kv_sem + 3)

    def key_value():
        kv_total = kv_out[half_own].astype(F32)
        for j in range(1, 4):
            wait(kv_in.at[j], kv_sem + j)
            kv_total = kv_total + kv_in[j].astype(F32)
        kv_total = jnp.where(c == 1, pltpu.roll(kv_total, HD // 2, 1), kv_total)
        low_lane = lax.broadcasted_iota(jnp.int32, (32, HD), 1) < HD // 2
        for j in range(2):
            part = jnp.where(
                low_lane,
                kv_total[64 * j : 64 * j + 32],
                pltpu.roll(kv_total[64 * j + 32 : 64 * j + 64], HD // 2, 1),
            )
            kv_all[0, x, :, j * HD : (j + 1) * HD] = part.astype(BF16)
        for j in (1, 3, 2):
            send(kv_all.at[0, x], kv_all.at[0, x], at_x(x + j), kvx + j)

    def kv_y_start():
        for j in range(1, NX):
            wait(kv_all.at[0, lax.rem(x + NX - j, NX)], kvx + j)
        kv_start()

    dx_up, dx_down, dx_up2, dx_down2 = new(8), new(8), new(8), new(8)
    head, tail = pl.ds(0, 64), pl.ds(64, 64)

    dy_up = {s: new() for s in range(1, 5)}
    dy_down = {s: new() for s in range(1, 5)}

    def d_receive(*steps):
        for i in steps:
            o = ORDER[i]
            mine = q_all.at[o, x]
            if o == 0:
                send(mine, q_all.at[7, x], y_up, dy_up[1])
                send(mine, q_all.at[1, x], y_down, dy_down[1])
            elif o == 4:
                wait(q_all.at[4, x, head], dy_up[4])
                wait(q_all.at[4, x, tail], dy_down[4])
            elif o < 4:
                wait(mine, dy_down[o])
                if o < 3:
                    send(mine, q_all.at[o + 1, x], y_down, dy_down[o + 1])
                else:
                    send(q_all.at[o, x, tail], q_all.at[4, x, tail], y_down, dy_down[4])
            else:
                wait(mine, dy_up[8 - o])
                if o > 5:
                    send(mine, q_all.at[o - 1, x], y_up, dy_up[9 - o])
                else:
                    send(q_all.at[o, x, head], q_all.at[4, x, head], y_up, dy_up[4])
            send(mine, mine, x_up, dx_up + i)
            send(mine, mine, x_down, dx_down + i)

    def d_forward(*steps):
        for i in steps:
            o = ORDER[i]
            wait(q_all.at[o, x_m], dx_up + i)
            send(q_all.at[o, x_m, head], q_all.at[o, x_m, head], x_up, dx_up2 + i)
            wait(q_all.at[o, x_p], dx_down + i)
            send(q_all.at[o, x_p, tail], q_all.at[o, x_p, tail], x_down, dx_down2 + i)

    sib_sem = new(8)

    def unpack(o, xx):
        raw = kv_all[o, xx].astype(F32)
        parts = []
        for j in range(2):
            part = raw[:, j * HD : (j + 1) * HD]
            parts += [part, pltpu.roll(part, HD // 2, 1)]
        return jnp.concatenate(parts, axis=0).astype(BF16)

    def d_terms(*steps):
        for i in steps:
            o = ORDER[i]
            wait(q_all.at[o, x_2, head], dx_up2 + i)
            wait(q_all.at[o, x_2, tail], dx_down2 + i)
            for xx in range(NX):
                kv_rows[o, xx] = unpack(o, xx)
            for own in (False, True):
                cc = c if own else 1 - c
                rows = dot_nt(q_all[o, pl.ds(2 * cc, 2)].reshape(BLOCK, BLOCK), wq_s[...])
                rows = rows + dot_nn(kv_rows[o, pl.ds(2 * cc, 2)].reshape(BLOCK, HD), w_kv[...])
                if own:
                    term_own[i] = rows
                else:
                    sib_out[i] = rows.astype(BF16)
                    send(sib_out.at[i], sib_in.at[i], sibling, sib_sem + i)

    def weights(*steps):
        for i in steps:
            o = ORDER[i]
            oz = lax.rem(y + o - z + NZ, NZ)
            for cc in range(2):
                acts = in_all[oz, cc]
                q_acc[...] += dot_nn(acts, q_all[o, 2 * cc : 2 * cc + 2].reshape(BLOCK, BLOCK))
                kv_acc[...] += dot_nn(acts, kv_rows[o, 2 * cc : 2 * cc + 2].reshape(BLOCK, HD))

    chain_send = new(16)
    chain_recv = new(64)
    halves = (pl.ds(0, PACK), pl.ds(PACK, PACK))

    def f_place(i):
        hops = lax.rem(y + ORDER[i] - z + NZ, NZ)
        return hops, (hops > 4).astype(jnp.int32)

    def f_send(i, slot, k, dev, order):
        part = pl.ds(pl.multiple_of(k * PACK, PACK), PACK)
        copy_of(
            chain_out.at[i, part],
            chain_in.at[i, slot, part],
            dev,
            chain_send + 2 * i + order,
            chain_recv + 8 * i + 2 * slot + k,
        ).start()

    def f_wait(i, slot, k):
        part = pl.ds(pl.multiple_of(k * PACK, PACK), PACK)
        wait(chain_in.at[i, slot, part], chain_recv + 8 * i + 2 * slot + k)
        return chain_in[i, slot, part, :].astype(F32)

    def f_sibling(*steps):
        for i in steps:
            f_first(i)

    def f_first(i):
        wait(sib_in.at[i], sib_sem + i)
        hops, side = f_place(i)
        total = term_own[i] + sib_in[i].astype(F32)
        term_own[i] = total

        @pl.when((hops != 0) & (hops != 2) & (hops != 6))
        def _():
            chain_out[i] = total.astype(BF16)

        @pl.when(hops == 4)
        def _():
            f_send(i, 1, 0, at_z(z + 2), 0)
            f_send(i, 1, 1, at_z(z + NZ - 2), 1)

        @pl.when((hops == 1) | (hops == 3) | (hops == 5) | (hops == 7))
        def _():
            slot = (hops == 7).astype(jnp.int32)
            for k in range(2):
                f_send(i, slot, k, at_z(z + 1 + side * (NZ - 2)), k)

    def f_middle(*steps):
        for i in steps:
            f_second(i)

    def f_second(i):
        hops, side = f_place(i)

        @pl.when((hops == 2) | (hops == 6))
        def _():
            for order in range(2):
                k = side if order == 0 else 1 - side
                part = pl.ds(pl.multiple_of(k * PACK, PACK), PACK)
                total = term_own[i, part, :] + f_wait(i, 0, k)
                if order == 0:
                    total = total + f_wait(i, 1, k)
                chain_out[i, part, :] = total.astype(BF16)
                f_send(i, 2 + side, k, at_z(z + 2 + side * (NZ - 4)), order)

    def f_owner(*steps):
        for i in steps:
            f_last(i)

    def f_last(i):
        hops, _ = f_place(i)

        @pl.when(hops == 0)
        def _():
            for k in range(2):
                total = term_own[i, halves[k], :]
                for slot in range(4):
                    total = total + f_wait(i, slot, k)
                fin[halves[k], :] = total

    def f_drain(i):
        hops, _ = f_place(i)

        @pl.when(hops != 0)
        def _():
            for k in range(2):
                like = chain_out.at[i, halves[k]]
                copy_of(like, like, sibling, chain_send + 2 * i + k, chain_recv).wait_send()

    def o_compute(*offsets):
        total = o_acc[...]
        for o in offsets:
            oz = lax.rem(y + o - z + NZ, NZ)
            for xx in range(NX):
                sub = (xx % 2) * PACK
                total = total + dot_nn(att_all[o, xx, 0 : 2 * HD, :], cot_all[oz, xx // 2, sub : sub + PACK, :])
        o_acc[...] = total

    loads[6].wait()
    rows_in(0)
    cot_step(1)
    tables()
    att_y_start()
    rows_in(1, 2)
    cot_step(2)
    b_forward(0)
    rows_in(3, 4)
    cot_step(3)
    b_forward(1)
    b_forward(2)
    b_finish(0)
    rows_in(5, 6)
    cot_step(4)
    in_start()
    b_forward(3)
    b_forward(4)
    rows_in(7)
    b_finish(1)
    b_finish(2)
    att_y_step(1)
    b_forward(5)
    b_forward(6)
    b_finish(3)
    b_finish(4)
    in_step(1)
    b_finish(5)
    b_finish(6)
    b_finish(7)
    in_step(2)
    backward()
    in_step(3)
    d_receive(1)
    key_value()
    d_receive(2)
    d_forward(0)
    kv_y_start()
    d_receive(3, 4)
    d_forward(1, 2)
    in_step(4)
    d_terms(0)
    kv_y_step(1)
    d_receive(5, 6)
    d_forward(3, 4)
    d_terms(1, 2)
    f_sibling(0)
    kv_y_step(2)
    d_receive(7)
    att_y_step(2)
    d_forward(5, 6)
    d_terms(3, 4)
    f_sibling(1, 2)
    kv_y_step(3)
    d_forward(7)
    d_terms(5, 6)
    f_sibling(3, 4)
    f_middle(0, 1, 2)
    kv_y_step(4)
    d_terms(7)
    f_sibling(5, 6)
    att_y_step(3)
    f_sibling(7)
    for o in range(8):
        in_sibling(o)
    weights(0, 1, 2, 3)
    f_middle(3, 4)
    weights(4, 5)
    f_middle(5, 6)
    weights(6, 7)
    f_middle(7)
    o_compute(0, 1, 7, 2, 6)
    f_owner(0, 1, 2, 3, 4, 5, 6)
    att_y_step(4)
    o_compute(3, 5, 4)
    f_owner(7)

    total = jnp.zeros((16, PACK), F32)
    for o in range(8):
        for xx in range(NX):
            total = total + att_all[o, xx, 2 * HD : ATT_ROWS, :].astype(F32)
    inv = 1.0 / total[0:1, 0:1]
    gin_ref[...] = (fin[...] * inv).astype(BF16)
    gq_ref[...] = (q_acc[...] * inv).astype(BF16)
    kv_sum = kv_acc[...] * inv
    kv_cols = kv_sum.T
    gk_ref[...] = kv_cols[0:32].astype(BF16)
    gv_ref[...] = kv_cols[32:64].astype(BF16)
    go_ref[...] = (o_acc[...] * inv).astype(BF16)

    for copy, when in drain:
        if when is None:
            copy.wait_send()
        else:
            (buf, i), sem = copy

            @pl.when(when)
            def _():
                like = buf.at[i, 0:PACK]
                copy_of(like, like, sibling, sem, sem).wait_send()

    for i in range(8):
        f_drain(i)
    assert used[0] <= SEMS, used[0]


SEMS = 384


def on_device(inputs, cotangent, queries, keys, values, lengths, counts, wq, wk, wv, wo):
    vmem = pl.BlockSpec(memory_space=pltpu.VMEM)
    hbm = pl.BlockSpec(memory_space=pltpu.HBM)
    sd = jax.ShapeDtypeStruct
    gin, gq, gk, gv, go = pl.pallas_call(
        kernel,
        out_shape=(
            sd((BLOCK, BLOCK), BF16),
            sd((BLOCK, BLOCK), BF16),
            sd((32, BLOCK), BF16),
            sd((32, BLOCK), BF16),
            sd((BLOCK, BLOCK), BF16),
        ),
        in_specs=[hbm] * 11,
        out_specs=(vmem,) * 5,
        scratch_shapes=[
            pltpu.VMEM((8, 2, BLOCK, BLOCK), BF16),
            pltpu.VMEM((8, 2, BLOCK, BLOCK), BF16),
            pltpu.VMEM((8, NX, ATT_ROWS, PACK), BF16),
            pltpu.VMEM((8, NX, PACK, BLOCK), BF16),
            pltpu.VMEM((8, NX, 32, BLOCK), BF16),
            pltpu.VMEM((8, NX, PACK, HD), BF16),
            pltpu.VMEM((8, PACK, BLOCK), BF16),
            pltpu.VMEM((8, NX, PACK, BLOCK), BF16),
            pltpu.VMEM((8, PACK, BLOCK), BF16),
            pltpu.VMEM((8, PACK, BLOCK), BF16),
            pltpu.VMEM((8, 64, BLOCK), F32),
            pltpu.VMEM((8, 64, BLOCK), F32),
            pltpu.VMEM((8, PACK, BLOCK), F32),
            pltpu.VMEM((8, 192, BLOCK), BF16),
            pltpu.VMEM((8, 192, BLOCK), BF16),
            pltpu.VMEM((8, 64, BLOCK), BF16),
            pltpu.VMEM((8, 64, BLOCK), BF16),
            pltpu.VMEM((8, PACK, BLOCK), BF16),
            pltpu.VMEM((8, PACK, BLOCK), BF16),
            pltpu.VMEM((PACK, BLOCK), F32),
            pltpu.VMEM((2, PACK, PACK), F32),
            pltpu.VMEM((2, PACK, HD), F32),
            pltpu.VMEM((PACK, HD), F32),
            pltpu.VMEM((PACK, HD), F32),
            pltpu.VMEM((2, PACK, HD), BF16),
            pltpu.VMEM((4, PACK, HD), BF16),
            pltpu.VMEM((HD, BLOCK), BF16),
            pltpu.VMEM((BLOCK, BLOCK), F32),
            pltpu.VMEM((BLOCK, HD), F32),
            pltpu.VMEM((BLOCK, BLOCK), F32),
            pltpu.VMEM((8, BLOCK, BLOCK), F32),
            pltpu.VMEM((8, BLOCK, BLOCK), BF16),
            pltpu.VMEM((8, BLOCK, BLOCK), BF16),
            pltpu.VMEM((8, BLOCK, BLOCK), BF16),
            pltpu.VMEM((8, 4, BLOCK, BLOCK), BF16),
            pltpu.VMEM((BLOCK, BLOCK), F32),
            pltpu.VMEM((BLOCK, BLOCK), BF16),
            pltpu.VMEM((PACK, BLOCK), BF16),
            pltpu.VMEM((PACK, HD), BF16),
            pltpu.VMEM((PACK, HD), BF16),
            pltpu.VMEM((BLOCK, BLOCK), BF16),
            pltpu.VMEM((BLOCK, BLOCK), BF16),
            pltpu.SMEM((1, DOCS), jnp.int32),
            pltpu.SMEM((1, 1), jnp.int32),
            pltpu.SemaphoreType.DMA((SEMS,)),
            pltpu.SemaphoreType.DMA((SEMS,)),
            pltpu.SemaphoreType.DMA((11,)),
        ],
        compiler_params=pltpu.CompilerParams(
            collective_id=0, has_side_effects=True, vmem_limit_bytes=60 * 1024 * 1024
        ),
        name="attention_block_backward",
    )(inputs, cotangent, queries, keys, values, lengths, counts.reshape(1, 1), wq, wk.T, wv.T, wo)
    return gin, gq, gk.T, gv.T, go


def solution(mesh):
    return jax.shard_map(
        on_device,
        mesh=mesh,
        in_specs=(
            P("tensor", "dp"),
            P("tensor", "dp"),
            P("dp", "tensor"),
            P("dp", None),
            P("dp", None),
            P("dp", None),
            P("dp"),
            P("dp", "tensor"),
            P("dp", "tensor"),
            P("dp", "tensor"),
            P("tensor", "dp"),
        ),
        out_specs=(
            P("tensor", "dp"),
            P("dp", "tensor"),
            P("dp", "tensor"),
            P("dp", "tensor"),
            P("tensor", "dp"),
        ),
        check_vma=False,
    )
```

```python
import math

import jax
import jax.numpy as jnp
from jax import lax
from jax.experimental import pallas as pl
from jax.experimental.pallas import tpu as pltpu
from jax.sharding import PartitionSpec as P

NX, NY, NZ = 4, 8, 8
HD = 128
PACK = 128
DOCS = 8
BLOCK = 256
THETA = 500000.0
ORDER = (0, 1, 7, 2, 6, 3, 5, 4)
ATT_ROWS = 2 * HD + 16
DIRECT = 7
F32 = jnp.float32
BF16 = jnp.bfloat16
NT = (((1,), (1,)), ((), ()))


def dot_nn(a, b):
    return jnp.dot(a, b, preferred_element_type=F32)


def dot_nt(a, b):
    return lax.dot_general(a, b, NT, preferred_element_type=F32)


def dot_tn(a, b):
    return dot_nn(a.astype(F32).T.astype(BF16), b)


def kernel(
    in_ref,
    cot_ref,
    q_ref,
    k_ref,
    v_ref,
    len_ref,
    cnt_ref,
    wq_ref,
    wk_ref,
    wv_ref,
    wo_ref,
    gin_ref,
    gq_ref,
    gk_ref,
    gv_ref,
    go_ref,
    cot_all,
    in_all,
    att_all,
    q_all,
    kv_all,
    kv_rows,
    x_out,
    x_in,
    b_right,
    b_left,
    keep_right,
    keep_left,
    keep_own,
    from_left,
    from_right,
    sum_right,
    sum_left,
    row_out,
    row_in,
    grad_own,
    probs_s,
    att_s,
    cos_s,
    sin_s,
    kv_out,
    kv_in,
    w_kv,
    q_acc,
    kv_acc,
    o_acc,
    term_own,
    sib_out,
    sib_in,
    chain_out,
    chain_in,
    fin,
    in_raw,
    q_s,
    k_s,
    v_s,
    wq_s,
    wo_s,
    len_s,
    cnt_s,
    send_sems,
    recv_sems,
    load_sems,
):
    d = lax.axis_index("dp")
    t = lax.axis_index("tensor")
    y, x = lax.div(d, NX), lax.rem(d, NX)
    z, c = lax.div(t, 2), lax.rem(t, 2)

    def at_z(zz, cc=c):
        return (d, lax.rem(zz, NZ) * 2 + cc)

    def at_x(xx):
        return (y * NX + lax.rem(xx, NX), t)

    def at_y(yy):
        return (lax.rem(yy, NY) * NX + x, t)

    sibling = (d, z * 2 + 1 - c)
    z_up, z_down = at_z(z + 1), at_z(z + NZ - 1)
    x_up, x_down = at_x(x + 1), at_x(x + NX - 1)
    y_up, y_down = at_y(y + 1), at_y(y + NY - 1)
    z_pair = z + 1 - 2 * lax.rem(z, 2)
    pair_same, pair_other = at_z(z_pair), at_z(z_pair, 1 - c)

    kv_head = pl.multiple_of(lax.div(t, 4) * HD, HD)
    head_cols = pl.ds(kv_head, HD)
    loads = [
        pltpu.make_async_copy(src, dst, load_sems.at[i])
        for i, (src, dst) in enumerate(
            (
                (cot_ref, cot_all.at[0, c]),
                (len_ref, len_s),
                (cnt_ref, cnt_s),
                (q_ref, q_s),
                (k_ref.at[:, head_cols], k_s),
                (v_ref.at[:, head_cols], v_s),
                (wo_ref, wo_s),
                (in_ref, in_raw),
                (wk_ref, w_kv.at[0:32]),
                (wv_ref, w_kv.at[32:64]),
                (wq_ref, wq_s),
            )
        )
    ]
    for load in loads:
        load.start()

    peers = [sibling, pair_other]
    peers += [at_x(x + j) for j in range(1, NX)]
    peers += [at_y(y + j) for j in range(1, NY)]
    peers += [at_z(z + j) for j in (1, 2, 6, 7)]
    barrier = pltpu.get_barrier_semaphore()
    for peer in peers:
        pl.semaphore_signal(barrier, inc=1, device_id=peer, device_id_type=pl.DeviceIdType.MESH)
    pl.semaphore_wait(barrier, len(peers))

    used = [0]
    drain = []

    def new(count=1):
        used[0] += count
        return used[0] - count

    def copy_of(src, dst, dev, si, ri):
        return pltpu.make_async_remote_copy(
            src_ref=src,
            dst_ref=dst,
            send_sem=send_sems.at[si],
            recv_sem=recv_sems.at[ri],
            device_id=dev,
            device_id_type=pl.DeviceIdType.MESH,
        )

    def send(src, dst, dev, ri, si=None, when=None, like=None):
        copy = copy_of(src, dst, dev, ri if si is None else si, ri)
        copy.start()
        if when is None:
            drain.append((copy, None))
        else:
            drain.append(((like, si), when))

    def wait(dst, ri, dev=sibling):
        copy_of(dst, dst, dev, ri, ri).wait_recv()

    def z_gather(buf, rows, chunks):
        size, half = rows // chunks, chunks // 2
        part = [pl.ds(k * size, size) for k in range(chunks)]
        up = {s: [new() for _ in range(chunks)] for s in range(1, 5)}
        down = {s: [new() for _ in range(chunks)] for s in range(1, 5)}
        sib = {o: (new(), new()) for o in range(8)}

        def to_sibling(o, k):
            both = buf.at[o, c, pl.ds(k * (rows // 2), rows // 2)]
            send(both, both, sibling, sib[o][k])

        def start():
            for k in range(chunks):
                own = buf.at[0, c, part[k]]
                send(own, buf.at[7, c, part[k]], z_up, up[1][k])
                send(own, buf.at[1, c, part[k]], z_down, down[1][k])
            for k in range(2):
                to_sibling(0, k)

        def step(s):
            lo, hi = (8 - s) % 8, s
            if s == 4:
                for k in range(chunks):
                    wait(buf.at[4, c, part[k]], (up if k < half else down)[4][k])
                    if (k + 1) % half == 0:
                        to_sibling(4, k // half)
                return
            order = [(o, k) for k in range(chunks) for o in (lo, hi)]
            if s == 3:
                order = [q for k in range(half) for q in ((lo, k), (hi, k + half))]
                order += [q for k in range(half) for q in ((lo, k + half), (hi, k))]
            for o, k in order:
                sems, dev, to = (up, z_up, o - 1) if o == lo else (down, z_down, o + 1)
                here = buf.at[o, c, part[k]]
                wait(here, sems[s][k])
                if s < 3 or (k < half) == (o == lo):
                    send(here, buf.at[to, c, part[k]], dev, sems[s + 1][k])
                if (k + 1) % half == 0:
                    to_sibling(o, k // half)

        def wait_sibling(o):
            for k in range(2):
                wait(buf.at[o, 1 - c, pl.ds(k * (rows // 2), rows // 2)], sib[o][k])

        return start, step, wait_sibling

    loads[0].wait()
    cot_start, cot_step, cot_sibling = z_gather(cot_all, BLOCK, 4)
    in_start, in_step, in_sibling = z_gather(in_all, BLOCK, 2)
    cot_start()

    for load in loads[1:6]:
        load.wait()
    rows_i = lax.broadcasted_iota(jnp.int32, (PACK, PACK), 0)
    cols_i = lax.broadcasted_iota(jnp.int32, (PACK, PACK), 1)
    end = 0
    doc_row = jnp.zeros((PACK, PACK), jnp.int32)
    doc_col = jnp.zeros((PACK, PACK), jnp.int32)
    first = jnp.zeros((PACK, PACK), jnp.int32)
    for j in range(DOCS):
        length = len_s[0, j]
        end = end + length
        passed = rows_i >= end
        doc_row = doc_row + passed.astype(jnp.int32)
        doc_col = doc_col + (cols_i >= end).astype(jnp.int32)
        first = first + jnp.where(passed, length, 0)
    allowed = (doc_row == doc_col) & (cols_i <= rows_i)
    scale = HD ** (-0.5)
    for h in range(2):
        scores = dot_nt(q_s[:, h * HD : (h + 1) * HD], k_s[...]) * scale
        scores = jnp.where(allowed, scores, -jnp.inf)
        exponent = jnp.exp(scores - jnp.max(scores, axis=1, keepdims=True))
        probs = exponent / jnp.sum(exponent, axis=1, keepdims=True)
        probs_s[h] = probs
        attended = dot_nn(probs.astype(BF16), v_s[...]).astype(BF16)
        att_s[h] = attended.astype(F32)
        att_all[0, x, h * HD : (h + 1) * HD, :] = attended.astype(F32).T.astype(BF16)
    count = cnt_s[0, 0].astype(F32)
    att_all[0, x, 2 * HD : ATT_ROWS, :] = jnp.full((16, PACK), 1.0, F32).astype(BF16) * jnp.full((16, PACK), count, F32).astype(BF16)

    ax = new(NX)
    for j in (1, 3, 2):
        send(att_all.at[0, x], att_all.at[0, x], at_x(x + j), ax + j)
    x_m, x_p, x_2 = lax.rem(x + 3, NX), lax.rem(x + 1, NX), lax.rem(x + 2, NX)

    def y_gather(buf):
        up = {s: (new(), new()) for s in range(1, 5)}
        down = {s: (new(), new()) for s in range(1, 5)}
        part = (pl.ds(0, 2), pl.ds(2, 2))

        def start():
            for k in range(2):
                send(buf.at[0, part[k]], buf.at[7, part[k]], y_up, up[1][k])
                send(buf.at[0, part[k]], buf.at[1, part[k]], y_down, down[1][k])

        def step(s, k):
            lo, hi = 8 - s, s
            if s == 4:
                wait(buf.at[4, part[k]], (up if k == 0 else down)[4][k])
                return
            wait(buf.at[lo, part[k]], up[s][k])
            if s < 3 or k == 0:
                send(buf.at[lo, part[k]], buf.at[lo - 1, part[k]], y_up, up[s + 1][k])
            wait(buf.at[hi, part[k]], down[s][k])
            if s < 3 or k == 1:
                send(buf.at[hi, part[k]], buf.at[hi + 1, part[k]], y_down, down[s + 1][k])

        return start, step

    att_start, att_y_step = y_gather(att_all)

    def att_y_start():
        for j in range(1, NX):
            wait(att_all.at[0, lax.rem(x + NX - j, NX)], ax + j)
        att_start()

    def tables():
        lane = jnp.where(cols_i < HD // 2, cols_i, cols_i - HD // 2)
        frequency = jnp.exp(lane.astype(F32) * (-2.0 * math.log(THETA) / HD))
        phases = (rows_i - first).astype(F32) * frequency
        cos_s[...] = jnp.cos(phases)
        sines = jnp.sin(phases)
        sin_s[...] = jnp.where(cols_i < HD // 2, sines, -sines)
        for load in loads[7:]:
            load.wait()
        in_all[0, c] = in_raw[...].astype(F32).T.astype(BF16)
        w_kv[64:128] = jnp.zeros((64, BLOCK), BF16)
        q_acc[...] = jnp.zeros_like(q_acc)
        kv_acc[...] = jnp.zeros_like(kv_acc)
        o_acc[...] = jnp.zeros_like(o_acc)

    bx_up, bx_down, bx_up2, bx_down2 = new(8), new(8), new(8), new(8)
    bx_far = new(8)
    by_send, by_recv = new(8), new(8)

    def b_terms(i):
        o = ORDER[i]

        def term(r):
            xx = lax.rem(x + r, NX)
            start = pl.multiple_of(lax.rem(xx, 2) * PACK, PACK)
            return dot_nt(cot_all[o, lax.div(xx, 2), pl.ds(start, PACK), :], wo_s[...])

        if i >= DIRECT:
            for r, buf, sem in ((2, x_out, bx_far), (1, b_right, bx_up), (3, b_left, bx_down)):
                buf[i] = term(r).astype(BF16)
                send(buf.at[i], x_in.at[i, r], at_x(x + r), sem + i)
            keep_own[i] = term(0)
            return
        far = term(2).astype(BF16)
        b_right[i, 0:64] = far[64:]
        b_left[i, 0:64] = far[:64]
        right = term(1)
        b_right[i, 64:128] = right[:64].astype(BF16)
        send(b_right.at[i], from_left.at[i, 0:128], x_up, bx_up + i)
        left = term(3)
        b_left[i, 64:128] = left[64:].astype(BF16)
        send(b_left.at[i], from_right.at[i, 0:128], x_down, bx_down + i)
        keep_right[i] = right[64:]
        keep_left[i] = left[:64]
        keep_own[i] = term(0)

    def b_forward(i):
        wait(from_left.at[i, 0:128], bx_up + i)
        sum_right[i] = (keep_right[i] + from_left[i, 0:64].astype(F32)).astype(BF16)
        send(sum_right.at[i], from_left.at[i, 128:192], x_up, bx_up2 + i)
        wait(from_right.at[i, 0:128], bx_down + i)
        sum_left[i] = (keep_left[i] + from_right[i, 0:64].astype(F32)).astype(BF16)
        send(sum_left.at[i], from_right.at[i, 128:192], x_down, bx_down2 + i)

    def b_finish(i):
        if i >= DIRECT:
            whole = keep_own[i]
            for r, sem in ((1, bx_up), (3, bx_down), (2, bx_far)):
                wait(x_in.at[i, r], sem + i)
                whole = whole + x_in[i, r].astype(F32)
            top, low = whole[0:64], whole[64:128]
        else:
            top, low = b_ring_sum(i)
        row = lax.rem(z + ORDER[i], NY)
        hops = lax.rem(row - y + NY, NY)

        @pl.when(hops == 0)
        def _():
            grad_own[0:64] = top
            grad_own[64:128] = low

        away = hops != 0

        @pl.when(away)
        def _():
            row_out[i, 0:64] = top.astype(BF16)
            row_out[i, 64:128] = low.astype(BF16)
            send(row_out.at[i], row_in.at[hops], at_y(row), by_recv + hops, by_send + i, away, (row_in, i))

    def b_ring_sum(i):
        wait(from_left.at[i, 128:192], bx_up2 + i)
        wait(from_right.at[i, 128:192], bx_down2 + i)
        top = keep_own[i, 0:64] + from_left[i, 64:128].astype(F32) + from_right[i, 128:192].astype(F32)
        low = keep_own[i, 64:128] + from_left[i, 128:192].astype(F32) + from_right[i, 64:128].astype(F32)
        return top, low

    def rows_in(*steps):
        for i in steps:
            cot_sibling(ORDER[i])
            b_terms(i)

    kv_sem, kvx, kvy = new(4), new(NX), new(8)
    half_own = lax.rem(z, 2)

    def rotate_back(value):
        return value * cos_s[...] + pltpu.roll(value, HD // 2, 1) * sin_s[...]

    def backward():
        grad = grad_own[...]
        for j in range(1, NY):
            wait(row_in.at[j], by_recv + j)
            grad = grad + row_in[j].astype(F32)
        grad_b = grad.astype(BF16)
        key_post = jnp.zeros((PACK, HD), F32)
        value_post = jnp.zeros((PACK, HD), F32)
        for h in range(2):
            grad_h = grad_b[:, h * HD : (h + 1) * HD]
            probs = probs_s[h]
            prob_grad = dot_nt(grad_h, v_s[...])
            row_dot = jnp.sum(grad_h.astype(F32) * att_s[h], axis=1, keepdims=True)
            score_grad = (probs * (prob_grad - row_dot)).astype(BF16)
            query_post = dot_nn(score_grad, k_s[...]) * scale
            q_all[0, x, :, h * HD : (h + 1) * HD] = rotate_back(query_post).astype(BF16)
            key_post = key_post + dot_tn(score_grad, q_s[:, h * HD : (h + 1) * HD]) * scale
            value_post = value_post + dot_tn(probs.astype(BF16), grad_h)
        d_receive(0)
        key_sum = rotate_back(key_post).astype(BF16)
        value_sum = value_post.astype(BF16)
        sel_r = lax.broadcasted_iota(jnp.int32, (HD, BLOCK), 0)
        sel_c = lax.broadcasted_iota(jnp.int32, (HD, BLOCK), 1)
        key_to = sel_r
        for edge in (32, 64, 96):
            key_to = key_to + 32 * (sel_r >= edge).astype(jnp.int32)
        packed = dot_nn(key_sum, (sel_c == key_to).astype(BF16)) + dot_nn(
            value_sum, (sel_c == key_to + 32).astype(BF16)
        )
        kv_out[0] = packed[:, :HD].astype(BF16)
        kv_out[1] = packed[:, HD:].astype(BF16)
        send(kv_out.at[half_own], kv_in.at[1], sibling, kv_sem + 1)
        send(kv_out.at[1 - half_own], kv_in.at[2], pair_same, kv_sem + 2)
        send(kv_out.at[1 - half_own], kv_in.at[3], pair_other, kv_sem + 3)

    def key_value():
        kv_total = kv_out[half_own].astype(F32)
        for j in range(1, 4):
            wait(kv_in.at[j], kv_sem + j)
            kv_total = kv_total + kv_in[j].astype(F32)
        kv_total = jnp.where(c == 1, pltpu.roll(kv_total, HD // 2, 1), kv_total)
        low_lane = lax.broadcasted_iota(jnp.int32, (32, HD), 1) < HD // 2
        for j in range(2):
            part = jnp.where(
                low_lane,
                kv_total[64 * j : 64 * j + 32],
                pltpu.roll(kv_total[64 * j + 32 : 64 * j + 64], HD // 2, 1),
            )
            kv_all[0, x, :, j * HD : (j + 1) * HD] = part.astype(BF16)
        for j in (1, 3, 2):
            send(kv_all.at[0, x], kv_all.at[0, x], at_x(x + j), kvx + j)

    def kv_y_start():
        for j in range(1, NX):
            wait(kv_all.at[0, lax.rem(x + NX - j, NX)], kvx + j)
        for j in ORDER[1:5]:
            send(kv_all.at[0], kv_all.at[8 - j], at_y(y + j), kvy + 8 - j)

    dx_up, dx_down, dx_up2, dx_down2 = new(8), new(8), new(8), new(8)
    head, tail = pl.ds(0, 64), pl.ds(64, 64)

    dy = new(8)

    dy_far, kvy_far = new(2), new(2)

    def far_along_y(buf, parts, sem, sem_far, o):
        if o in (1, 7):
            to = 3 if o == 1 else 5
            dev = at_y(y + 6) if o == 1 else at_y(y + 2)
            send(buf(o), buf(to), dev, sem + to)
        elif o in (2, 6):
            k = 1 if o == 2 else 0
            dev = at_y(y + 6) if o == 2 else at_y(y + 2)
            send(buf(o).at[parts[k]], buf(4).at[parts[k]], dev, sem_far + k)

    def wait_along_y(buf, parts, sem, sem_far, o):
        if o == 4:
            for k in range(2):
                wait(buf(4).at[parts[k]], sem_far + k)
        elif o:
            wait(buf(o), sem + o)

    def d_receive(*steps):
        for i in steps:
            o = ORDER[i]
            mine = q_all.at[o, x]
            q_at = (lambda r: q_all.at[r, x], (head, tail), dy, dy_far, o)
            wait_along_y(*q_at)
            far_along_y(*q_at)
            send(mine, mine, x_up, dx_up + i)
            send(mine, mine, x_down, dx_down + i)
            if o == 0:
                for j in ORDER[1:5]:
                    send(mine, q_all.at[8 - j, x], at_y(y + j), dy + 8 - j)

    def kv_far(*offsets):
        for o in offsets:
            kv_at = (lambda r: kv_all.at[r], (pl.ds(0, 2), pl.ds(2, 2)), kvy, kvy_far, o)
            wait_along_y(*kv_at)
            far_along_y(*kv_at)

    def d_forward(*steps):
        for i in steps:
            o = ORDER[i]
            wait(q_all.at[o, x_m], dx_up + i)
            send(q_all.at[o, x_m, head], q_all.at[o, x_m, head], x_up, dx_up2 + i)
            wait(q_all.at[o, x_p], dx_down + i)
            send(q_all.at[o, x_p, tail], q_all.at[o, x_p, tail], x_down, dx_down2 + i)

    sib_sem = new(8)

    def unpack(o, xx):
        raw = kv_all[o, xx].astype(F32)
        parts = []
        for j in range(2):
            part = raw[:, j * HD : (j + 1) * HD]
            parts += [part, pltpu.roll(part, HD // 2, 1)]
        return jnp.concatenate(parts, axis=0).astype(BF16)

    def d_terms(*steps):
        for i in steps:
            o = ORDER[i]
            wait(q_all.at[o, x_2, head], dx_up2 + i)
            wait(q_all.at[o, x_2, tail], dx_down2 + i)
            if o in (3, 4, 5):
                kv_far(o)
            for xx in range(NX):
                kv_rows[o, xx] = unpack(o, xx)
            for own in (False, True):
                cc = c if own else 1 - c
                rows = dot_nt(q_all[o, pl.ds(2 * cc, 2)].reshape(BLOCK, BLOCK), wq_s[...])
                rows = rows + dot_nn(kv_rows[o, pl.ds(2 * cc, 2)].reshape(BLOCK, HD), w_kv[...])
                if own:
                    term_own[i] = rows
                else:
                    sib_out[i] = rows.astype(BF16)
                    send(sib_out.at[i], sib_in.at[i], sibling, sib_sem + i)

    def weights(*steps):
        for i in steps:
            o = ORDER[i]
            oz = lax.rem(y + o - z + NZ, NZ)
            for cc in range(2):
                acts = in_all[oz, cc]
                q_acc[...] += dot_nn(acts, q_all[o, 2 * cc : 2 * cc + 2].reshape(BLOCK, BLOCK))
                kv_acc[...] += dot_nn(acts, kv_rows[o, 2 * cc : 2 * cc + 2].reshape(BLOCK, HD))

    chain_send = new(16)
    chain_recv = new(64)
    halves = (pl.ds(0, PACK), pl.ds(PACK, PACK))

    def f_place(i):
        hops = lax.rem(y + ORDER[i] - z + NZ, NZ)
        return hops, (hops > 4).astype(jnp.int32)

    def f_send(i, slot, k, dev, order):
        part = pl.ds(pl.multiple_of(k * PACK, PACK), PACK)
        copy_of(
            chain_out.at[i, part],
            chain_in.at[i, slot, part],
            dev,
            chain_send + 2 * i + order,
            chain_recv + 8 * i + 2 * slot + k,
        ).start()

    def f_wait(i, slot, k):
        part = pl.ds(pl.multiple_of(k * PACK, PACK), PACK)
        wait(chain_in.at[i, slot, part], chain_recv + 8 * i + 2 * slot + k)
        return chain_in[i, slot, part, :].astype(F32)

    def f_sibling(*steps):
        for i in steps:
            f_first(i)

    def f_first(i):
        wait(sib_in.at[i], sib_sem + i)
        hops, side = f_place(i)
        total = term_own[i] + sib_in[i].astype(F32)
        term_own[i] = total

        @pl.when((hops != 0) & (hops != 2) & (hops != 6))
        def _():
            chain_out[i] = total.astype(BF16)

        @pl.when(hops == 4)
        def _():
            f_send(i, 1, 0, at_z(z + 2), 0)
            f_send(i, 1, 1, at_z(z + NZ - 2), 1)

        @pl.when((hops == 1) | (hops == 3) | (hops == 5) | (hops == 7))
        def _():
            slot = (hops == 7).astype(jnp.int32)
            for k in range(2):
                f_send(i, slot, k, at_z(z + 1 + side * (NZ - 2)), k)

    def f_middle(*steps):
        for i in steps:
            f_second(i)

    def f_second(i):
        hops, side = f_place(i)

        @pl.when((hops == 2) | (hops == 6))
        def _():
            for order in range(2):
                k = side if order == 0 else 1 - side
                part = pl.ds(pl.multiple_of(k * PACK, PACK), PACK)
                total = term_own[i, part, :] + f_wait(i, 0, k)
                if order == 0:
                    total = total + f_wait(i, 1, k)
                chain_out[i, part, :] = total.astype(BF16)
                f_send(i, 2 + side, k, at_z(z + 2 + side * (NZ - 4)), order)

    def f_owner(*steps):
        for i in steps:
            f_last(i)

    def f_last(i):
        hops, _ = f_place(i)

        @pl.when(hops == 0)
        def _():
            for k in range(2):
                total = term_own[i, halves[k], :]
                for slot in range(4):
                    total = total + f_wait(i, slot, k)
                fin[halves[k], :] = total

    def f_drain(i):
        hops, _ = f_place(i)

        @pl.when(hops != 0)
        def _():
            for k in range(2):
                like = chain_out.at[i, halves[k]]
                copy_of(like, like, sibling, chain_send + 2 * i + k, chain_recv).wait_send()

    def o_compute(*offsets):
        total = o_acc[...]
        for o in offsets:
            oz = lax.rem(y + o - z + NZ, NZ)
            for xx in range(NX):
                sub = (xx % 2) * PACK
                total = total + dot_nn(att_all[o, xx, 0 : 2 * HD, :], cot_all[oz, xx // 2, sub : sub + PACK, :])
        o_acc[...] = total

    loads[6].wait()
    rows_in(0)
    cot_step(1)
    tables()
    att_y_start()
    rows_in(1, 2)
    cot_step(2)
    b_forward(0)
    rows_in(3, 4)
    att_y_step(1, 0)
    cot_step(3)
    b_forward(1)
    b_forward(2)
    b_finish(0)
    att_y_step(1, 1)
    rows_in(5, 6)
    cot_step(4)
    in_start()
    att_y_step(2, 0)
    b_forward(3)
    b_forward(4)
    b_finish(1)
    b_finish(2)
    b_forward(5)
    b_forward(6)
    rows_in(7)
    b_finish(3)
    b_finish(4)
    in_step(1)
    b_finish(5)
    b_finish(6)
    b_finish(7)
    backward()
    key_value()
    d_receive(1, 2)
    d_forward(0)
    kv_y_start()
    in_step(2)
    d_receive(3, 4)
    d_forward(1, 2)
    kv_far(1, 7)
    d_receive(5, 6)
    d_terms(0)
    kv_far(2, 6)
    in_step(3)
    d_forward(3, 4)
    d_receive(7)
    d_terms(1, 2)
    f_sibling(0)
    d_forward(5, 6)
    att_y_step(2, 1)
    d_terms(3, 4)
    d_forward(7)
    in_step(4)
    f_sibling(1, 2)
    att_y_step(3, 0)
    d_terms(5, 6)
    f_sibling(3, 4)
    d_terms(7)
    f_middle(0, 1, 2)
    f_sibling(5, 6)
    f_sibling(7)
    att_y_step(3, 1)
    for o in range(8):
        in_sibling(o)
    weights(0, 1)
    f_middle(3, 4)
    weights(2, 3)
    f_middle(5, 6)
    f_middle(7)
    weights(4, 5, 6, 7)
    o_compute(0, 1, 7, 2, 6, 3, 5)
    f_owner(0, 1, 2, 3, 4, 5, 6)
    att_y_step(4, 0)
    att_y_step(4, 1)
    o_compute(4)
    f_owner(7)

    total = jnp.zeros((16, PACK), F32)
    for o in range(8):
        for xx in range(NX):
            total = total + att_all[o, xx, 2 * HD : ATT_ROWS, :].astype(F32)
    inv = 1.0 / total[0:1, 0:1]
    gin_ref[...] = (fin[...] * inv).astype(BF16)
    gq_ref[...] = (q_acc[...] * inv).astype(BF16)
    kv_sum = kv_acc[...] * inv
    kv_cols = kv_sum.T
    gk_ref[...] = kv_cols[0:32].astype(BF16)
    gv_ref[...] = kv_cols[32:64].astype(BF16)
    go_ref[...] = (o_acc[...] * inv).astype(BF16)

    for copy, when in drain:
        if when is None:
            copy.wait_send()
        else:
            (buf, i), sem = copy

            @pl.when(when)
            def _():
                like = buf.at[i, 0:PACK]
                copy_of(like, like, sibling, sem, sem).wait_send()

    for i in range(8):
        f_drain(i)
    assert used[0] <= SEMS, used[0]


SEMS = 384


def hand_over(*refs):
    srcs, dsts, sems = refs[:5], refs[5:10], refs[10]
    copies = [pltpu.make_async_copy(src, dst, sems.at[i]) for i, (src, dst) in enumerate(zip(srcs, dsts))]
    for copy in copies:
        copy.start()
    for copy in copies:
        copy.wait()


def on_device(inputs, cotangent, queries, keys, values, lengths, counts, wq, wk, wv, wo):
    vmem = pl.BlockSpec(memory_space=pltpu.VMEM)
    hbm = pl.BlockSpec(memory_space=pltpu.HBM)
    sd = jax.ShapeDtypeStruct
    shapes = (
        sd((BLOCK, BLOCK), BF16),
        sd((BLOCK, BLOCK), BF16),
        sd((32, BLOCK), BF16),
        sd((32, BLOCK), BF16),
        sd((BLOCK, BLOCK), BF16),
    )
    results = pl.pallas_call(
        kernel,
        out_shape=shapes,
        in_specs=[hbm] * 11,
        out_specs=(vmem,) * 5,
        scratch_shapes=[
            pltpu.VMEM((8, 2, BLOCK, BLOCK), BF16),
            pltpu.VMEM((8, 2, BLOCK, BLOCK), BF16),
            pltpu.VMEM((8, NX, ATT_ROWS, PACK), BF16),
            pltpu.VMEM((8, NX, PACK, BLOCK), BF16),
            pltpu.VMEM((8, NX, 32, BLOCK), BF16),
            pltpu.VMEM((8, NX, PACK, HD), BF16),
            pltpu.VMEM((8, PACK, BLOCK), BF16),
            pltpu.VMEM((8, NX, PACK, BLOCK), BF16),
            pltpu.VMEM((8, PACK, BLOCK), BF16),
            pltpu.VMEM((8, PACK, BLOCK), BF16),
            pltpu.VMEM((8, 64, BLOCK), F32),
            pltpu.VMEM((8, 64, BLOCK), F32),
            pltpu.VMEM((8, PACK, BLOCK), F32),
            pltpu.VMEM((8, 192, BLOCK), BF16),
            pltpu.VMEM((8, 192, BLOCK), BF16),
            pltpu.VMEM((8, 64, BLOCK), BF16),
            pltpu.VMEM((8, 64, BLOCK), BF16),
            pltpu.VMEM((8, PACK, BLOCK), BF16),
            pltpu.VMEM((8, PACK, BLOCK), BF16),
            pltpu.VMEM((PACK, BLOCK), F32),
            pltpu.VMEM((2, PACK, PACK), F32),
            pltpu.VMEM((2, PACK, HD), F32),
            pltpu.VMEM((PACK, HD), F32),
            pltpu.VMEM((PACK, HD), F32),
            pltpu.VMEM((2, PACK, HD), BF16),
            pltpu.VMEM((4, PACK, HD), BF16),
            pltpu.VMEM((HD, BLOCK), BF16),
            pltpu.VMEM((BLOCK, BLOCK), F32),
            pltpu.VMEM((BLOCK, HD), F32),
            pltpu.VMEM((BLOCK, BLOCK), F32),
            pltpu.VMEM((8, BLOCK, BLOCK), F32),
            pltpu.VMEM((8, BLOCK, BLOCK), BF16),
            pltpu.VMEM((8, BLOCK, BLOCK), BF16),
            pltpu.VMEM((8, BLOCK, BLOCK), BF16),
            pltpu.VMEM((8, 4, BLOCK, BLOCK), BF16),
            pltpu.VMEM((BLOCK, BLOCK), F32),
            pltpu.VMEM((BLOCK, BLOCK), BF16),
            pltpu.VMEM((PACK, BLOCK), BF16),
            pltpu.VMEM((PACK, HD), BF16),
            pltpu.VMEM((PACK, HD), BF16),
            pltpu.VMEM((BLOCK, BLOCK), BF16),
            pltpu.VMEM((BLOCK, BLOCK), BF16),
            pltpu.SMEM((1, DOCS), jnp.int32),
            pltpu.SMEM((1, 1), jnp.int32),
            pltpu.SemaphoreType.DMA((SEMS,)),
            pltpu.SemaphoreType.DMA((SEMS,)),
            pltpu.SemaphoreType.DMA((11,)),
        ],
        compiler_params=pltpu.CompilerParams(
            collective_id=0, has_side_effects=True, vmem_limit_bytes=60 * 1024 * 1024
        ),
        name="attention_block_backward",
    )(inputs, cotangent, queries, keys, values, lengths, counts.reshape(1, 1), wq, wk.T, wv.T, wo)
    gin, gq, gk, gv, go = pl.pallas_call(
        hand_over,
        out_shape=shapes,
        in_specs=[hbm] * 5,
        out_specs=(hbm,) * 5,
        scratch_shapes=[pltpu.SemaphoreType.DMA((5,))],
        compiler_params=pltpu.CompilerParams(vmem_limit_bytes=60 * 1024 * 1024),
        name="hand_over",
    )(*results)
    return gin, gq, gk.T, gv.T, go


def solution(mesh):
    return jax.shard_map(
        on_device,
        mesh=mesh,
        in_specs=(
            P("tensor", "dp"),
            P("tensor", "dp"),
            P("dp", "tensor"),
            P("dp", None),
            P("dp", None),
            P("dp", None),
            P("dp"),
            P("dp", "tensor"),
            P("dp", "tensor"),
            P("dp", "tensor"),
            P("tensor", "dp"),
        ),
        out_specs=(
            P("tensor", "dp"),
            P("dp", "tensor"),
            P("dp", "tensor"),
            P("dp", "tensor"),
            P("tensor", "dp"),
        ),
        check_vma=False,
    )
```

```python
import math

import jax
import jax.numpy as jnp
from jax import lax
from jax.experimental import pallas as pl
from jax.experimental.pallas import tpu as pltpu
from jax.sharding import PartitionSpec as P

NX, NY, NZ = 4, 8, 8
HD = 128
PACK = 128
DOCS = 8
BLOCK = 256
THETA = 500000.0
ORDER = (0, 1, 7, 2, 6, 3, 5, 4)
ATT_ROWS = 2 * HD + 16
DIRECT = 7
F32 = jnp.float32
BF16 = jnp.bfloat16
NT = (((1,), (1,)), ((), ()))


def dot_nn(a, b):
    return jnp.dot(a, b, preferred_element_type=F32)


def dot_nt(a, b):
    return lax.dot_general(a, b, NT, preferred_element_type=F32)


def dot_tn(a, b):
    return dot_nn(a.astype(F32).T.astype(BF16), b)


def kernel(
    in_ref,
    cot_ref,
    q_ref,
    k_ref,
    v_ref,
    len_ref,
    cnt_ref,
    wq_ref,
    wk_ref,
    wv_ref,
    wo_ref,
    gin_ref,
    gq_ref,
    gk_ref,
    gv_ref,
    go_ref,
    cot_all,
    in_all,
    att_all,
    q_all,
    kv_all,
    kv_rows,
    x_out,
    x_in,
    b_right,
    b_left,
    keep_right,
    keep_left,
    keep_own,
    from_left,
    from_right,
    sum_right,
    sum_left,
    row_out,
    row_in,
    grad_own,
    probs_s,
    probs_t,
    select,
    att_s,
    cos_s,
    sin_s,
    kv_out,
    kv_in,
    w_kv,
    q_acc,
    kv_acc,
    o_acc,
    term_own,
    sib_out,
    sib_in,
    chain_out,
    chain_in,
    fin,
    in_raw,
    q_s,
    k_s,
    v_s,
    wq_s,
    wo_s,
    len_s,
    cnt_s,
    send_sems,
    recv_sems,
    load_sems,
):
    d = lax.axis_index("dp")
    t = lax.axis_index("tensor")
    y, x = lax.div(d, NX), lax.rem(d, NX)
    z, c = lax.div(t, 2), lax.rem(t, 2)

    def at_z(zz, cc=c):
        return (d, lax.rem(zz, NZ) * 2 + cc)

    def at_x(xx):
        return (y * NX + lax.rem(xx, NX), t)

    def at_y(yy):
        return (lax.rem(yy, NY) * NX + x, t)

    sibling = (d, z * 2 + 1 - c)
    z_up, z_down = at_z(z + 1), at_z(z + NZ - 1)
    x_up, x_down = at_x(x + 1), at_x(x + NX - 1)
    y_up, y_down = at_y(y + 1), at_y(y + NY - 1)
    z_pair = z + 1 - 2 * lax.rem(z, 2)
    pair_same, pair_other = at_z(z_pair), at_z(z_pair, 1 - c)

    kv_head = pl.multiple_of(lax.div(t, 4) * HD, HD)
    head_cols = pl.ds(kv_head, HD)
    loads = [
        pltpu.make_async_copy(src, dst, load_sems.at[i])
        for i, (src, dst) in enumerate(
            (
                (cot_ref, cot_all.at[0, c]),
                (len_ref, len_s),
                (cnt_ref, cnt_s),
                (q_ref, q_s),
                (k_ref.at[:, head_cols], k_s),
                (v_ref.at[:, head_cols], v_s),
                (wo_ref, wo_s),
                (in_ref, in_raw),
                (wk_ref, w_kv.at[0:32]),
                (wv_ref, w_kv.at[32:64]),
                (wq_ref, wq_s),
            )
        )
    ]
    for load in loads:
        load.start()

    peers = [sibling, pair_other]
    peers += [at_x(x + j) for j in range(1, NX)]
    peers += [at_y(y + j) for j in range(1, NY)]
    peers += [at_z(z + j) for j in (1, 2, 6, 7)]
    barrier = pltpu.get_barrier_semaphore()
    for peer in peers:
        pl.semaphore_signal(barrier, inc=1, device_id=peer, device_id_type=pl.DeviceIdType.MESH)
    pl.semaphore_wait(barrier, len(peers))

    used = [0]
    drain = []

    def new(count=1):
        used[0] += count
        return used[0] - count

    def copy_of(src, dst, dev, si, ri):
        return pltpu.make_async_remote_copy(
            src_ref=src,
            dst_ref=dst,
            send_sem=send_sems.at[si],
            recv_sem=recv_sems.at[ri],
            device_id=dev,
            device_id_type=pl.DeviceIdType.MESH,
        )

    def send(src, dst, dev, ri, si=None, when=None, like=None):
        copy = copy_of(src, dst, dev, ri if si is None else si, ri)
        copy.start()
        if when is None:
            drain.append((copy, None))
        else:
            drain.append(((like, si), when))

    def wait(dst, ri, dev=sibling):
        copy_of(dst, dst, dev, ri, ri).wait_recv()

    def z_gather(buf, rows, chunks):
        size, half = rows // chunks, chunks // 2
        part = [pl.ds(k * size, size) for k in range(chunks)]
        up = {s: [new() for _ in range(chunks)] for s in range(1, 5)}
        down = {s: [new() for _ in range(chunks)] for s in range(1, 5)}
        sib = {o: (new(), new()) for o in range(8)}

        def to_sibling(o, k):
            both = buf.at[o, c, pl.ds(k * (rows // 2), rows // 2)]
            send(both, both, sibling, sib[o][k])

        def start():
            for k in range(chunks):
                own = buf.at[0, c, part[k]]
                send(own, buf.at[7, c, part[k]], z_up, up[1][k])
                send(own, buf.at[1, c, part[k]], z_down, down[1][k])
            for k in range(2):
                to_sibling(0, k)

        def step(s):
            lo, hi = (8 - s) % 8, s
            if s == 4:
                for k in range(chunks):
                    wait(buf.at[4, c, part[k]], (up if k < half else down)[4][k])
                    if (k + 1) % half == 0:
                        to_sibling(4, k // half)
                return
            order = [(o, k) for k in range(chunks) for o in (lo, hi)]
            if s == 3:
                order = [q for k in range(half) for q in ((lo, k), (hi, k + half))]
                order += [q for k in range(half) for q in ((lo, k + half), (hi, k))]
            for o, k in order:
                sems, dev, to = (up, z_up, o - 1) if o == lo else (down, z_down, o + 1)
                here = buf.at[o, c, part[k]]
                wait(here, sems[s][k])
                if s < 3 or (k < half) == (o == lo):
                    send(here, buf.at[to, c, part[k]], dev, sems[s + 1][k])
                if (k + 1) % half == 0:
                    to_sibling(o, k // half)

        def wait_sibling(o):
            for k in range(2):
                wait(buf.at[o, 1 - c, pl.ds(k * (rows // 2), rows // 2)], sib[o][k])

        return start, step, wait_sibling

    loads[0].wait()
    cot_start, cot_step, cot_sibling = z_gather(cot_all, BLOCK, 4)
    in_start, in_step, in_sibling = z_gather(in_all, BLOCK, 2)
    cot_start()

    for load in loads[1:6]:
        load.wait()
    rows_i = lax.broadcasted_iota(jnp.int32, (PACK, PACK), 0)
    cols_i = lax.broadcasted_iota(jnp.int32, (PACK, PACK), 1)
    end = 0
    doc_row = jnp.zeros((PACK, PACK), jnp.int32)
    doc_col = jnp.zeros((PACK, PACK), jnp.int32)
    first = jnp.zeros((PACK, PACK), jnp.int32)
    for j in range(DOCS):
        length = len_s[0, j]
        end = end + length
        passed = rows_i >= end
        doc_row = doc_row + passed.astype(jnp.int32)
        doc_col = doc_col + (cols_i >= end).astype(jnp.int32)
        first = first + jnp.where(passed, length, 0)
    allowed = (doc_row == doc_col) & (cols_i <= rows_i)
    scale = HD ** (-0.5)
    for h in range(2):
        scores = dot_nt(q_s[:, h * HD : (h + 1) * HD], k_s[...]) * scale
        scores = jnp.where(allowed, scores, -jnp.inf)
        exponent = jnp.exp(scores - jnp.max(scores, axis=1, keepdims=True))
        probs = exponent / jnp.sum(exponent, axis=1, keepdims=True)
        probs_s[h] = probs
        attended = dot_nn(probs.astype(BF16), v_s[...]).astype(BF16)
        att_s[h] = attended.astype(F32)
        att_all[0, x, h * HD : (h + 1) * HD, :] = attended.astype(F32).T.astype(BF16)
    count = cnt_s[0, 0].astype(F32)
    att_all[0, x, 2 * HD : ATT_ROWS, :] = jnp.full((16, PACK), 1.0, F32).astype(BF16) * jnp.full((16, PACK), count, F32).astype(BF16)

    ax = new(NX)
    for j in (1, 3, 2):
        send(att_all.at[0, x], att_all.at[0, x], at_x(x + j), ax + j)
    x_m, x_p, x_2 = lax.rem(x + 3, NX), lax.rem(x + 1, NX), lax.rem(x + 2, NX)

    def y_gather(buf):
        up = {s: (new(), new()) for s in range(1, 5)}
        down = {s: (new(), new()) for s in range(1, 5)}
        part = (pl.ds(0, 2), pl.ds(2, 2))

        def start():
            for k in range(2):
                send(buf.at[0, part[k]], buf.at[7, part[k]], y_up, up[1][k])
                send(buf.at[0, part[k]], buf.at[1, part[k]], y_down, down[1][k])

        def step(s, k):
            lo, hi = 8 - s, s
            if s == 4:
                wait(buf.at[4, part[k]], (up if k == 0 else down)[4][k])
                return
            wait(buf.at[lo, part[k]], up[s][k])
            if s < 3 or k == 0:
                send(buf.at[lo, part[k]], buf.at[lo - 1, part[k]], y_up, up[s + 1][k])
            wait(buf.at[hi, part[k]], down[s][k])
            if s < 3 or k == 1:
                send(buf.at[hi, part[k]], buf.at[hi + 1, part[k]], y_down, down[s + 1][k])

        return start, step

    att_start, att_y_step = y_gather(att_all)

    def att_y_start():
        for j in range(1, NX):
            wait(att_all.at[0, lax.rem(x + NX - j, NX)], ax + j)
        att_start()

    def tables():
        lane = jnp.where(cols_i < HD // 2, cols_i, cols_i - HD // 2)
        frequency = jnp.exp(lane.astype(F32) * (-2.0 * math.log(THETA) / HD))
        phases = (rows_i - first).astype(F32) * frequency
        cos_s[...] = jnp.cos(phases)
        sines = jnp.sin(phases)
        sin_s[...] = jnp.where(cols_i < HD // 2, sines, -sines)
        for load in loads[7:]:
            load.wait()
        in_all[0, c] = in_raw[...].astype(F32).T.astype(BF16)
        w_kv[64:128] = jnp.zeros((64, BLOCK), BF16)
        sel_r = lax.broadcasted_iota(jnp.int32, (HD, BLOCK), 0)
        sel_c = lax.broadcasted_iota(jnp.int32, (HD, BLOCK), 1)
        key_to = sel_r
        for edge in (32, 64, 96):
            key_to = key_to + 32 * (sel_r >= edge).astype(jnp.int32)
        select[0] = (sel_c == key_to).astype(BF16)
        select[1] = (sel_c == key_to + 32).astype(BF16)
        for h in range(2):
            probs_t[h] = probs_s[h].astype(BF16).astype(F32).T.astype(BF16)
        q_acc[...] = jnp.zeros_like(q_acc)
        kv_acc[...] = jnp.zeros_like(kv_acc)
        o_acc[...] = jnp.zeros_like(o_acc)

    bx_up, bx_down, bx_up2, bx_down2 = new(8), new(8), new(8), new(8)
    bx_far = new(8)
    by_send, by_recv = new(8), new(8)

    def b_terms(i):
        o = ORDER[i]

        def term(r):
            xx = lax.rem(x + r, NX)
            start = pl.multiple_of(lax.rem(xx, 2) * PACK, PACK)
            return dot_nt(cot_all[o, lax.div(xx, 2), pl.ds(start, PACK), :], wo_s[...])

        if i >= DIRECT:
            for r, buf, sem in ((2, x_out, bx_far), (1, b_right, bx_up), (3, b_left, bx_down)):
                buf[i] = term(r).astype(BF16)
                send(buf.at[i], x_in.at[i, r], at_x(x + r), sem + i)
            keep_own[i] = term(0)
            return
        far = term(2).astype(BF16)
        b_right[i, 0:64] = far[64:]
        b_left[i, 0:64] = far[:64]
        right = term(1)
        b_right[i, 64:128] = right[:64].astype(BF16)
        send(b_right.at[i], from_left.at[i, 0:128], x_up, bx_up + i)
        left = term(3)
        b_left[i, 64:128] = left[64:].astype(BF16)
        send(b_left.at[i], from_right.at[i, 0:128], x_down, bx_down + i)
        keep_right[i] = right[64:]
        keep_left[i] = left[:64]
        keep_own[i] = term(0)

    def b_forward(i):
        wait(from_left.at[i, 0:128], bx_up + i)
        sum_right[i] = (keep_right[i] + from_left[i, 0:64].astype(F32)).astype(BF16)
        send(sum_right.at[i], from_left.at[i, 128:192], x_up, bx_up2 + i)
        wait(from_right.at[i, 0:128], bx_down + i)
        sum_left[i] = (keep_left[i] + from_right[i, 0:64].astype(F32)).astype(BF16)
        send(sum_left.at[i], from_right.at[i, 128:192], x_down, bx_down2 + i)

    def b_finish(i):
        if i >= DIRECT:
            whole = keep_own[i]
            for r, sem in ((1, bx_up), (3, bx_down), (2, bx_far)):
                wait(x_in.at[i, r], sem + i)
                whole = whole + x_in[i, r].astype(F32)
            top, low = whole[0:64], whole[64:128]
        else:
            top, low = b_ring_sum(i)
        row = lax.rem(z + ORDER[i], NY)
        hops = lax.rem(row - y + NY, NY)

        @pl.when(hops == 0)
        def _():
            grad_own[0:64] = top
            grad_own[64:128] = low

        away = hops != 0

        @pl.when(away)
        def _():
            row_out[i, 0:64] = top.astype(BF16)
            row_out[i, 64:128] = low.astype(BF16)
            send(row_out.at[i], row_in.at[hops], at_y(row), by_recv + hops, by_send + i, away, (row_in, i))

    def b_ring_sum(i):
        wait(from_left.at[i, 128:192], bx_up2 + i)
        wait(from_right.at[i, 128:192], bx_down2 + i)
        top = keep_own[i, 0:64] + from_left[i, 64:128].astype(F32) + from_right[i, 128:192].astype(F32)
        low = keep_own[i, 64:128] + from_left[i, 128:192].astype(F32) + from_right[i, 64:128].astype(F32)
        return top, low

    def rows_in(*steps):
        for i in steps:
            cot_sibling(ORDER[i])
            b_terms(i)

    kv_sem, kvx, kvy = new(4), new(NX), new(8)
    half_own = lax.rem(z, 2)

    def rotate_back(value):
        return value * cos_s[...] + pltpu.roll(value, HD // 2, 1) * sin_s[...]

    def backward():
        grad = grad_own[...]
        for j in range(1, NY):
            wait(row_in.at[j], by_recv + j)
            grad = grad + row_in[j].astype(F32)
        grad_b = grad.astype(BF16)
        kept = []
        for h in range(2):
            grad_h = grad_b[:, h * HD : (h + 1) * HD]
            probs = probs_s[h]
            prob_grad = dot_nt(grad_h, v_s[...])
            row_dot = jnp.sum(grad_h.astype(F32) * att_s[h], axis=1, keepdims=True)
            score_grad = (probs * (prob_grad - row_dot)).astype(BF16)
            query_post = dot_nn(score_grad, k_s[...]) * scale
            q_all[0, x, :, h * HD : (h + 1) * HD] = rotate_back(query_post).astype(BF16)
            kept.append((grad_h, score_grad))
        d_receive(0)
        key_post = jnp.zeros((PACK, HD), F32)
        value_post = jnp.zeros((PACK, HD), F32)
        for h, (grad_h, score_grad) in enumerate(kept):
            key_post = key_post + dot_tn(score_grad, q_s[:, h * HD : (h + 1) * HD]) * scale
            value_post = value_post + dot_nn(probs_t[h], grad_h)
        key_sum = rotate_back(key_post).astype(BF16)
        value_sum = value_post.astype(BF16)
        packed = dot_nn(key_sum, select[0]) + dot_nn(value_sum, select[1])
        kv_out[0] = packed[:, :HD].astype(BF16)
        kv_out[1] = packed[:, HD:].astype(BF16)
        send(kv_out.at[half_own], kv_in.at[1], sibling, kv_sem + 1)
        send(kv_out.at[1 - half_own], kv_in.at[2], pair_same, kv_sem + 2)
        send(kv_out.at[1 - half_own], kv_in.at[3], pair_other, kv_sem + 3)

    def key_value():
        kv_total = kv_out[half_own].astype(F32)
        for j in range(1, 4):
            wait(kv_in.at[j], kv_sem + j)
            kv_total = kv_total + kv_in[j].astype(F32)
        kv_total = jnp.where(c == 1, pltpu.roll(kv_total, HD // 2, 1), kv_total)
        low_lane = lax.broadcasted_iota(jnp.int32, (32, HD), 1) < HD // 2
        for j in range(2):
            part = jnp.where(
                low_lane,
                kv_total[64 * j : 64 * j + 32],
                pltpu.roll(kv_total[64 * j + 32 : 64 * j + 64], HD // 2, 1),
            )
            kv_all[0, x, :, j * HD : (j + 1) * HD] = part.astype(BF16)
        for j in (1, 3, 2):
            send(kv_all.at[0, x], kv_all.at[0, x], at_x(x + j), kvx + j)

    def kv_y_start():
        for j in range(1, NX):
            wait(kv_all.at[0, lax.rem(x + NX - j, NX)], kvx + j)
        for j in ORDER[1:5]:
            send(kv_all.at[0], kv_all.at[8 - j], at_y(y + j), kvy + 8 - j)

    dx_up, dx_down, dx_up2, dx_down2 = new(8), new(8), new(8), new(8)
    head, tail = pl.ds(0, 64), pl.ds(64, 64)

    dy = new(8)

    dy_far, kvy_far = new(2), new(2)

    def far_along_y(buf, parts, sem, sem_far, o):
        if o in (1, 7):
            to = 3 if o == 1 else 5
            dev = at_y(y + 6) if o == 1 else at_y(y + 2)
            send(buf(o), buf(to), dev, sem + to)
        elif o in (2, 6):
            k = 1 if o == 2 else 0
            dev = at_y(y + 6) if o == 2 else at_y(y + 2)
            send(buf(o).at[parts[k]], buf(4).at[parts[k]], dev, sem_far + k)

    def wait_along_y(buf, parts, sem, sem_far, o):
        if o == 4:
            for k in range(2):
                wait(buf(4).at[parts[k]], sem_far + k)
        elif o:
            wait(buf(o), sem + o)

    def d_receive(*steps):
        for i in steps:
            o = ORDER[i]
            mine = q_all.at[o, x]
            q_at = (lambda r: q_all.at[r, x], (head, tail), dy, dy_far, o)
            wait_along_y(*q_at)
            far_along_y(*q_at)
            send(mine, mine, x_up, dx_up + i)
            send(mine, mine, x_down, dx_down + i)
            if o == 0:
                for j in ORDER[1:5]:
                    send(mine, q_all.at[8 - j, x], at_y(y + j), dy + 8 - j)

    def kv_far(*offsets):
        for o in offsets:
            kv_at = (lambda r: kv_all.at[r], (pl.ds(0, 2), pl.ds(2, 2)), kvy, kvy_far, o)
            wait_along_y(*kv_at)
            far_along_y(*kv_at)

    def d_forward(*steps):
        for i in steps:
            o = ORDER[i]
            wait(q_all.at[o, x_m], dx_up + i)
            send(q_all.at[o, x_m, head], q_all.at[o, x_m, head], x_up, dx_up2 + i)
            wait(q_all.at[o, x_p], dx_down + i)
            send(q_all.at[o, x_p, tail], q_all.at[o, x_p, tail], x_down, dx_down2 + i)

    sib_sem = new(8)

    def unpack(o, xx):
        raw = kv_all[o, xx].astype(F32)
        parts = []
        for j in range(2):
            part = raw[:, j * HD : (j + 1) * HD]
            parts += [part, pltpu.roll(part, HD // 2, 1)]
        return jnp.concatenate(parts, axis=0).astype(BF16)

    def d_terms(*steps):
        for i in steps:
            o = ORDER[i]
            wait(q_all.at[o, x_2, head], dx_up2 + i)
            wait(q_all.at[o, x_2, tail], dx_down2 + i)
            if o in (3, 4, 5):
                kv_far(o)
            for xx in range(NX):
                kv_rows[o, xx] = unpack(o, xx)
            for own in (False, True):
                cc = c if own else 1 - c
                rows = dot_nt(q_all[o, pl.ds(2 * cc, 2)].reshape(BLOCK, BLOCK), wq_s[...])
                rows = rows + dot_nn(kv_rows[o, pl.ds(2 * cc, 2)].reshape(BLOCK, HD), w_kv[...])
                if own:
                    term_own[i] = rows
                else:
                    sib_out[i] = rows.astype(BF16)
                    send(sib_out.at[i], sib_in.at[i], sibling, sib_sem + i)

    def weights(*steps):
        for i in steps:
            o = ORDER[i]
            oz = lax.rem(y + o - z + NZ, NZ)
            for cc in range(2):
                acts = in_all[oz, cc]
                q_acc[...] += dot_nn(acts, q_all[o, 2 * cc : 2 * cc + 2].reshape(BLOCK, BLOCK))
                kv_acc[...] += dot_nn(acts, kv_rows[o, 2 * cc : 2 * cc + 2].reshape(BLOCK, HD))

    chain_send = new(16)
    chain_recv = new(64)
    halves = (pl.ds(0, PACK), pl.ds(PACK, PACK))

    def f_place(i):
        hops = lax.rem(y + ORDER[i] - z + NZ, NZ)
        return hops, (hops > 4).astype(jnp.int32)

    def f_send(i, slot, k, dev, order):
        part = pl.ds(pl.multiple_of(k * PACK, PACK), PACK)
        copy_of(
            chain_out.at[i, part],
            chain_in.at[i, slot, part],
            dev,
            chain_send + 2 * i + order,
            chain_recv + 8 * i + 2 * slot + k,
        ).start()

    def f_wait(i, slot, k):
        part = pl.ds(pl.multiple_of(k * PACK, PACK), PACK)
        wait(chain_in.at[i, slot, part], chain_recv + 8 * i + 2 * slot + k)
        return chain_in[i, slot, part, :].astype(F32)

    def f_sibling(*steps):
        for i in steps:
            f_first(i)

    def f_first(i):
        wait(sib_in.at[i], sib_sem + i)
        hops, side = f_place(i)
        total = term_own[i] + sib_in[i].astype(F32)
        term_own[i] = total

        @pl.when((hops != 0) & (hops != 2) & (hops != 6))
        def _():
            chain_out[i] = total.astype(BF16)

        @pl.when(hops == 4)
        def _():
            f_send(i, 1, 0, at_z(z + 2), 0)
            f_send(i, 1, 1, at_z(z + NZ - 2), 1)

        @pl.when((hops == 1) | (hops == 3) | (hops == 5) | (hops == 7))
        def _():
            slot = (hops == 7).astype(jnp.int32)
            for k in range(2):
                f_send(i, slot, k, at_z(z + 1 + side * (NZ - 2)), k)

    def f_middle(*steps):
        for i in steps:
            f_second(i)

    def f_second(i):
        hops, side = f_place(i)

        @pl.when((hops == 2) | (hops == 6))
        def _():
            for order in range(2):
                k = side if order == 0 else 1 - side
                part = pl.ds(pl.multiple_of(k * PACK, PACK), PACK)
                total = term_own[i, part, :] + f_wait(i, 0, k)
                if order == 0:
                    total = total + f_wait(i, 1, k)
                chain_out[i, part, :] = total.astype(BF16)
                f_send(i, 2 + side, k, at_z(z + 2 + side * (NZ - 4)), order)

    def f_owner(*steps):
        for i in steps:
            f_last(i)

    def f_last(i):
        hops, _ = f_place(i)

        @pl.when(hops == 0)
        def _():
            for k in range(2):
                total = term_own[i, halves[k], :]
                for slot in range(4):
                    total = total + f_wait(i, slot, k)
                fin[halves[k], :] = total

    def f_drain(i):
        hops, _ = f_place(i)

        @pl.when(hops != 0)
        def _():
            for k in range(2):
                like = chain_out.at[i, halves[k]]
                copy_of(like, like, sibling, chain_send + 2 * i + k, chain_recv).wait_send()

    def o_compute(*offsets):
        total = o_acc[...]
        for o in offsets:
            oz = lax.rem(y + o - z + NZ, NZ)
            for xx in range(NX):
                sub = (xx % 2) * PACK
                total = total + dot_nn(att_all[o, xx, 0 : 2 * HD, :], cot_all[oz, xx // 2, sub : sub + PACK, :])
        o_acc[...] = total

    loads[6].wait()
    rows_in(0)
    cot_step(1)
    tables()
    att_y_start()
    rows_in(1, 2)
    cot_step(2)
    b_forward(0)
    rows_in(3, 4)
    att_y_step(1, 0)
    cot_step(3)
    b_forward(1)
    b_forward(2)
    b_finish(0)
    att_y_step(1, 1)
    rows_in(5, 6)
    cot_step(4)
    in_start()
    att_y_step(2, 0)
    b_forward(3)
    b_forward(4)
    b_finish(1)
    b_finish(2)
    b_forward(5)
    b_forward(6)
    rows_in(7)
    b_finish(3)
    b_finish(4)
    in_step(1)
    b_finish(5)
    b_finish(6)
    b_finish(7)
    backward()
    key_value()
    d_receive(1, 2)
    d_forward(0)
    kv_y_start()
    in_step(2)
    d_receive(3, 4)
    d_forward(1, 2)
    kv_far(1, 7)
    d_receive(5, 6)
    d_terms(0)
    kv_far(2, 6)
    in_step(3)
    d_forward(3, 4)
    d_receive(7)
    d_terms(1, 2)
    f_sibling(0)
    d_forward(5, 6)
    att_y_step(2, 1)
    d_terms(3, 4)
    d_forward(7)
    in_step(4)
    f_sibling(1, 2)
    att_y_step(3, 0)
    d_terms(5, 6)
    f_sibling(3, 4)
    d_terms(7)
    f_middle(0, 1, 2)
    f_sibling(5, 6)
    f_sibling(7)
    att_y_step(3, 1)
    for o in range(8):
        in_sibling(o)
    weights(0, 1)
    f_middle(3, 4)
    weights(2, 3)
    f_middle(5, 6)
    f_middle(7)
    weights(4, 5, 6, 7)
    o_compute(0, 1, 7, 2, 6, 3, 5)
    f_owner(0, 1, 2, 3, 4, 5, 6)
    att_y_step(4, 0)
    att_y_step(4, 1)
    o_compute(4)
    f_owner(7)

    total = jnp.zeros((16, PACK), F32)
    for o in range(8):
        for xx in range(NX):
            total = total + att_all[o, xx, 2 * HD : ATT_ROWS, :].astype(F32)
    inv = 1.0 / total[0:1, 0:1]
    gin_ref[...] = (fin[...] * inv).astype(BF16)
    gq_ref[...] = (q_acc[...] * inv).astype(BF16)
    kv_sum = kv_acc[...] * inv
    kv_cols = kv_sum.T
    gk_ref[...] = kv_cols[0:32].astype(BF16)
    gv_ref[...] = kv_cols[32:64].astype(BF16)
    go_ref[...] = (o_acc[...] * inv).astype(BF16)

    for copy, when in drain:
        if when is None:
            copy.wait_send()
        else:
            (buf, i), sem = copy

            @pl.when(when)
            def _():
                like = buf.at[i, 0:PACK]
                copy_of(like, like, sibling, sem, sem).wait_send()

    for i in range(8):
        f_drain(i)
    assert used[0] <= SEMS, used[0]


SEMS = 384


def hand_over(*refs):
    srcs, dsts, bufs, sems = refs[:5], refs[5:10], refs[10:15], refs[15]
    loads = [pltpu.make_async_copy(a, b, sems.at[0, i]) for i, (a, b) in enumerate(zip(srcs, bufs))]
    stores = [pltpu.make_async_copy(a, b, sems.at[1, i]) for i, (a, b) in enumerate(zip(bufs, dsts))]
    for load in loads:
        load.start()
    for load, store in zip(loads, stores):
        load.wait()
        store.start()
    for store in stores:
        store.wait()


def on_device(inputs, cotangent, queries, keys, values, lengths, counts, wq, wk, wv, wo):
    vmem = pl.BlockSpec(memory_space=pltpu.VMEM)
    hbm = pl.BlockSpec(memory_space=pltpu.HBM)
    sd = jax.ShapeDtypeStruct
    shapes = (
        sd((BLOCK, BLOCK), BF16),
        sd((BLOCK, BLOCK), BF16),
        sd((32, BLOCK), BF16),
        sd((32, BLOCK), BF16),
        sd((BLOCK, BLOCK), BF16),
    )
    results = pl.pallas_call(
        kernel,
        out_shape=shapes,
        in_specs=[hbm] * 11,
        out_specs=(vmem,) * 5,
        scratch_shapes=[
            pltpu.VMEM((8, 2, BLOCK, BLOCK), BF16),
            pltpu.VMEM((8, 2, BLOCK, BLOCK), BF16),
            pltpu.VMEM((8, NX, ATT_ROWS, PACK), BF16),
            pltpu.VMEM((8, NX, PACK, BLOCK), BF16),
            pltpu.VMEM((8, NX, 32, BLOCK), BF16),
            pltpu.VMEM((8, NX, PACK, HD), BF16),
            pltpu.VMEM((8, PACK, BLOCK), BF16),
            pltpu.VMEM((8, NX, PACK, BLOCK), BF16),
            pltpu.VMEM((8, PACK, BLOCK), BF16),
            pltpu.VMEM((8, PACK, BLOCK), BF16),
            pltpu.VMEM((8, 64, BLOCK), F32),
            pltpu.VMEM((8, 64, BLOCK), F32),
            pltpu.VMEM((8, PACK, BLOCK), F32),
            pltpu.VMEM((8, 192, BLOCK), BF16),
            pltpu.VMEM((8, 192, BLOCK), BF16),
            pltpu.VMEM((8, 64, BLOCK), BF16),
            pltpu.VMEM((8, 64, BLOCK), BF16),
            pltpu.VMEM((8, PACK, BLOCK), BF16),
            pltpu.VMEM((8, PACK, BLOCK), BF16),
            pltpu.VMEM((PACK, BLOCK), F32),
            pltpu.VMEM((2, PACK, PACK), F32),
            pltpu.VMEM((2, PACK, PACK), BF16),
            pltpu.VMEM((2, HD, BLOCK), BF16),
            pltpu.VMEM((2, PACK, HD), F32),
            pltpu.VMEM((PACK, HD), F32),
            pltpu.VMEM((PACK, HD), F32),
            pltpu.VMEM((2, PACK, HD), BF16),
            pltpu.VMEM((4, PACK, HD), BF16),
            pltpu.VMEM((HD, BLOCK), BF16),
            pltpu.VMEM((BLOCK, BLOCK), F32),
            pltpu.VMEM((BLOCK, HD), F32),
            pltpu.VMEM((BLOCK, BLOCK), F32),
            pltpu.VMEM((8, BLOCK, BLOCK), F32),
            pltpu.VMEM((8, BLOCK, BLOCK), BF16),
            pltpu.VMEM((8, BLOCK, BLOCK), BF16),
            pltpu.VMEM((8, BLOCK, BLOCK), BF16),
            pltpu.VMEM((8, 4, BLOCK, BLOCK), BF16),
            pltpu.VMEM((BLOCK, BLOCK), F32),
            pltpu.VMEM((BLOCK, BLOCK), BF16),
            pltpu.VMEM((PACK, BLOCK), BF16),
            pltpu.VMEM((PACK, HD), BF16),
            pltpu.VMEM((PACK, HD), BF16),
            pltpu.VMEM((BLOCK, BLOCK), BF16),
            pltpu.VMEM((BLOCK, BLOCK), BF16),
            pltpu.SMEM((1, DOCS), jnp.int32),
            pltpu.SMEM((1, 1), jnp.int32),
            pltpu.SemaphoreType.DMA((SEMS,)),
            pltpu.SemaphoreType.DMA((SEMS,)),
            pltpu.SemaphoreType.DMA((11,)),
        ],
        compiler_params=pltpu.CompilerParams(
            collective_id=0, has_side_effects=True, vmem_limit_bytes=60 * 1024 * 1024
        ),
        name="attention_block_backward",
    )(inputs, cotangent, queries, keys, values, lengths, counts.reshape(1, 1), wq, wk.T, wv.T, wo)
    gin, gq, gk, gv, go = pl.pallas_call(
        hand_over,
        out_shape=shapes,
        in_specs=[hbm] * 5,
        out_specs=(hbm,) * 5,
        scratch_shapes=[pltpu.VMEM(a.shape, a.dtype) for a in shapes] + [pltpu.SemaphoreType.DMA((2, 5))],
        compiler_params=pltpu.CompilerParams(vmem_limit_bytes=60 * 1024 * 1024),
        name="hand_over",
    )(*results)
    return gin, gq, gk.T, gv.T, go


def solution(mesh):
    return jax.shard_map(
        on_device,
        mesh=mesh,
        in_specs=(
            P("tensor", "dp"),
            P("tensor", "dp"),
            P("dp", "tensor"),
            P("dp", None),
            P("dp", None),
            P("dp", None),
            P("dp"),
            P("dp", "tensor"),
            P("dp", "tensor"),
            P("dp", "tensor"),
            P("tensor", "dp"),
        ),
        out_specs=(
            P("tensor", "dp"),
            P("dp", "tensor"),
            P("dp", "tensor"),
            P("dp", "tensor"),
            P("tensor", "dp"),
        ),
        check_vma=False,
    )
```

```python
import math

import jax
import jax.numpy as jnp
from jax import lax
from jax.experimental import pallas as pl
from jax.experimental.pallas import tpu as pltpu
from jax.sharding import PartitionSpec as P

NX, NY, NZ = 4, 8, 8
HD = 128
PACK = 128
DOCS = 8
BLOCK = 256
THETA = 500000.0
ORDER = (0, 1, 7, 2, 6, 3, 5, 4)
ATT_ROWS = 2 * HD + 16
DIRECT = 7
F32 = jnp.float32
BF16 = jnp.bfloat16
NT = (((1,), (1,)), ((), ()))


def dot_nn(a, b):
    return jnp.dot(a, b, preferred_element_type=F32)


def dot_nt(a, b):
    return lax.dot_general(a, b, NT, preferred_element_type=F32)


def dot_tn(a, b):
    return dot_nn(a.astype(F32).T.astype(BF16), b)


def kernel(
    in_ref,
    cot_ref,
    q_ref,
    k_ref,
    v_ref,
    len_ref,
    cnt_ref,
    wq_ref,
    wk_ref,
    wv_ref,
    wo_ref,
    gin_ref,
    gq_ref,
    gk_ref,
    gv_ref,
    go_ref,
    cot_all,
    in_all,
    att_all,
    q_all,
    kv_all,
    kv_rows,
    x_out,
    x_in,
    b_right,
    b_left,
    keep_right,
    keep_left,
    keep_own,
    from_left,
    from_right,
    sum_right,
    sum_left,
    row_out,
    row_in,
    grad_own,
    probs_s,
    probs_t,
    select,
    att_s,
    cos_s,
    sin_s,
    kv_out,
    kv_in,
    w_kv,
    q_acc,
    kv_acc,
    o_acc,
    term_own,
    sib_out,
    sib_in,
    chain_out,
    chain_in,
    fin,
    in_raw,
    q_s,
    k_s,
    v_s,
    wq_s,
    wo_s,
    len_s,
    cnt_s,
    send_sems,
    recv_sems,
    load_sems,
):
    d = lax.axis_index("dp")
    t = lax.axis_index("tensor")
    y, x = lax.div(d, NX), lax.rem(d, NX)
    z, c = lax.div(t, 2), lax.rem(t, 2)

    def at_z(zz, cc=c):
        return (d, lax.rem(zz, NZ) * 2 + cc)

    def at_x(xx):
        return (y * NX + lax.rem(xx, NX), t)

    def at_y(yy):
        return (lax.rem(yy, NY) * NX + x, t)

    sibling = (d, z * 2 + 1 - c)
    z_up, z_down = at_z(z + 1), at_z(z + NZ - 1)
    x_up, x_down = at_x(x + 1), at_x(x + NX - 1)
    y_up, y_down = at_y(y + 1), at_y(y + NY - 1)
    z_pair = z + 1 - 2 * lax.rem(z, 2)
    pair_same, pair_other = at_z(z_pair), at_z(z_pair, 1 - c)

    kv_head = pl.multiple_of(lax.div(t, 4) * HD, HD)
    head_cols = pl.ds(kv_head, HD)
    loads = [
        pltpu.make_async_copy(src, dst, load_sems.at[i])
        for i, (src, dst) in enumerate(
            (
                (cot_ref, cot_all.at[0, c]),
                (len_ref, len_s),
                (cnt_ref, cnt_s),
                (q_ref, q_s),
                (k_ref.at[:, head_cols], k_s),
                (v_ref.at[:, head_cols], v_s),
                (wo_ref, wo_s),
                (in_ref, in_raw),
                (wk_ref, w_kv.at[0:32]),
                (wv_ref, w_kv.at[32:64]),
                (wq_ref, wq_s),
            )
        )
    ]
    for load in loads:
        load.start()

    peers = [sibling, pair_other]
    peers += [at_x(x + j) for j in range(1, NX)]
    peers += [at_y(y + j) for j in range(1, NY)]
    peers += [at_z(z + j) for j in (1, 2, 6, 7)]
    barrier = pltpu.get_barrier_semaphore()
    for peer in peers:
        pl.semaphore_signal(barrier, inc=1, device_id=peer, device_id_type=pl.DeviceIdType.MESH)
    pl.semaphore_wait(barrier, len(peers))

    used = [0]
    drain = []

    def new(count=1):
        used[0] += count
        return used[0] - count

    def copy_of(src, dst, dev, si, ri):
        return pltpu.make_async_remote_copy(
            src_ref=src,
            dst_ref=dst,
            send_sem=send_sems.at[si],
            recv_sem=recv_sems.at[ri],
            device_id=dev,
            device_id_type=pl.DeviceIdType.MESH,
        )

    def send(src, dst, dev, ri, si=None, when=None, like=None):
        copy = copy_of(src, dst, dev, ri if si is None else si, ri)
        copy.start()
        if when is None:
            drain.append((copy, None))
        else:
            drain.append(((like, si), when))

    def wait(dst, ri, dev=sibling):
        copy_of(dst, dst, dev, ri, ri).wait_recv()

    def z_gather(buf, rows, chunks):
        size, half = rows // chunks, chunks // 2
        part = [pl.ds(k * size, size) for k in range(chunks)]
        up = {s: [new() for _ in range(chunks)] for s in range(1, 5)}
        down = {s: [new() for _ in range(chunks)] for s in range(1, 5)}
        sib = {o: (new(), new()) for o in range(8)}

        def to_sibling(o, k):
            both = buf.at[o, c, pl.ds(k * (rows // 2), rows // 2)]
            send(both, both, sibling, sib[o][k])

        def start():
            for k in range(chunks):
                own = buf.at[0, c, part[k]]
                send(own, buf.at[7, c, part[k]], z_up, up[1][k])
                send(own, buf.at[1, c, part[k]], z_down, down[1][k])
            for k in range(2):
                to_sibling(0, k)

        def step(s):
            lo, hi = (8 - s) % 8, s
            if s == 4:
                for k in range(chunks):
                    wait(buf.at[4, c, part[k]], (up if k < half else down)[4][k])
                    if (k + 1) % half == 0:
                        to_sibling(4, k // half)
                return
            order = [(o, k) for k in range(chunks) for o in (lo, hi)]
            if s == 3:
                order = [q for k in range(half) for q in ((lo, k), (hi, k + half))]
                order += [q for k in range(half) for q in ((lo, k + half), (hi, k))]
            for o, k in order:
                sems, dev, to = (up, z_up, o - 1) if o == lo else (down, z_down, o + 1)
                here = buf.at[o, c, part[k]]
                wait(here, sems[s][k])
                if s < 3 or (k < half) == (o == lo):
                    send(here, buf.at[to, c, part[k]], dev, sems[s + 1][k])
                if (k + 1) % half == 0:
                    to_sibling(o, k // half)

        def wait_sibling(o):
            for k in range(2):
                wait(buf.at[o, 1 - c, pl.ds(k * (rows // 2), rows // 2)], sib[o][k])

        return start, step, wait_sibling

    loads[0].wait()
    cot_start, cot_step, cot_sibling = z_gather(cot_all, BLOCK, 4)
    in_start, in_step, in_sibling = z_gather(in_all, BLOCK, 2)
    cot_start()

    for load in loads[1:6]:
        load.wait()
    rows_i = lax.broadcasted_iota(jnp.int32, (PACK, PACK), 0)
    cols_i = lax.broadcasted_iota(jnp.int32, (PACK, PACK), 1)
    end = 0
    doc_row = jnp.zeros((PACK, PACK), jnp.int32)
    doc_col = jnp.zeros((PACK, PACK), jnp.int32)
    first = jnp.zeros((PACK, PACK), jnp.int32)
    for j in range(DOCS):
        length = len_s[0, j]
        end = end + length
        passed = rows_i >= end
        doc_row = doc_row + passed.astype(jnp.int32)
        doc_col = doc_col + (cols_i >= end).astype(jnp.int32)
        first = first + jnp.where(passed, length, 0)
    allowed = (doc_row == doc_col) & (cols_i <= rows_i)
    scale = HD ** (-0.5)
    for h in range(2):
        scores = dot_nt(q_s[:, h * HD : (h + 1) * HD], k_s[...]) * scale
        scores = jnp.where(allowed, scores, -jnp.inf)
        exponent = jnp.exp(scores - jnp.max(scores, axis=1, keepdims=True))
        probs = exponent / jnp.sum(exponent, axis=1, keepdims=True)
        probs_s[h] = probs
        attended = dot_nn(probs.astype(BF16), v_s[...]).astype(BF16)
        att_s[h] = attended.astype(F32)
        att_all[0, x, h * HD : (h + 1) * HD, :] = attended.astype(F32).T.astype(BF16)
    count = cnt_s[0, 0].astype(F32)
    att_all[0, x, 2 * HD : ATT_ROWS, :] = jnp.full((16, PACK), 1.0, F32).astype(BF16) * jnp.full((16, PACK), count, F32).astype(BF16)

    ax = new(NX)
    for j in (1, 3, 2):
        send(att_all.at[0, x], att_all.at[0, x], at_x(x + j), ax + j)
    x_m, x_p, x_2 = lax.rem(x + 3, NX), lax.rem(x + 1, NX), lax.rem(x + 2, NX)

    def y_gather(buf):
        up = {s: (new(), new()) for s in range(1, 5)}
        down = {s: (new(), new()) for s in range(1, 5)}
        part = (pl.ds(0, 2), pl.ds(2, 2))

        def start():
            for k in range(2):
                send(buf.at[0, part[k]], buf.at[7, part[k]], y_up, up[1][k])
                send(buf.at[0, part[k]], buf.at[1, part[k]], y_down, down[1][k])

        def step(s, k):
            lo, hi = 8 - s, s
            if s == 4:
                wait(buf.at[4, part[k]], (up if k == 0 else down)[4][k])
                return
            wait(buf.at[lo, part[k]], up[s][k])
            if s < 3 or k == 0:
                send(buf.at[lo, part[k]], buf.at[lo - 1, part[k]], y_up, up[s + 1][k])
            wait(buf.at[hi, part[k]], down[s][k])
            if s < 3 or k == 1:
                send(buf.at[hi, part[k]], buf.at[hi + 1, part[k]], y_down, down[s + 1][k])

        return start, step

    att_start, att_y_step = y_gather(att_all)

    def att_y_start():
        for j in range(1, NX):
            wait(att_all.at[0, lax.rem(x + NX - j, NX)], ax + j)
        att_start()

    def tables():
        lane = jnp.where(cols_i < HD // 2, cols_i, cols_i - HD // 2)
        frequency = jnp.exp(lane.astype(F32) * (-2.0 * math.log(THETA) / HD))
        phases = (rows_i - first).astype(F32) * frequency
        cos_s[...] = jnp.cos(phases)
        sines = jnp.sin(phases)
        sin_s[...] = jnp.where(cols_i < HD // 2, sines, -sines)
        for load in loads[7:]:
            load.wait()
        in_all[0, c] = in_raw[...].astype(F32).T.astype(BF16)
        w_kv[64:128] = jnp.zeros((64, BLOCK), BF16)
        sel_r = lax.broadcasted_iota(jnp.int32, (HD, BLOCK), 0)
        sel_c = lax.broadcasted_iota(jnp.int32, (HD, BLOCK), 1)
        key_to = sel_r
        for edge in (32, 64, 96):
            key_to = key_to + 32 * (sel_r >= edge).astype(jnp.int32)
        select[0] = (sel_c == key_to).astype(BF16)
        select[1] = (sel_c == key_to + 32).astype(BF16)
        for h in range(2):
            probs_t[h] = probs_s[h].astype(BF16).astype(F32).T.astype(BF16)
        q_acc[...] = jnp.zeros_like(q_acc)
        kv_acc[...] = jnp.zeros_like(kv_acc)
        o_acc[...] = jnp.zeros_like(o_acc)

    bx_up, bx_down, bx_up2, bx_down2 = new(8), new(8), new(8), new(8)
    bx_far = new(8)
    by_send, by_recv = new(8), new(8)

    def b_terms(i):
        o = ORDER[i]

        def term(r):
            xx = lax.rem(x + r, NX)
            start = pl.multiple_of(lax.rem(xx, 2) * PACK, PACK)
            return dot_nt(cot_all[o, lax.div(xx, 2), pl.ds(start, PACK), :], wo_s[...])

        if i >= DIRECT:
            for r, buf, sem in ((2, x_out, bx_far), (1, b_right, bx_up), (3, b_left, bx_down)):
                buf[i] = term(r).astype(BF16)
                send(buf.at[i], x_in.at[i, r], at_x(x + r), sem + i)
            keep_own[i] = term(0)
            return
        far = term(2).astype(BF16)
        b_right[i, 0:64] = far[64:]
        b_left[i, 0:64] = far[:64]
        right = term(1)
        b_right[i, 64:128] = right[:64].astype(BF16)
        send(b_right.at[i], from_left.at[i, 0:128], x_up, bx_up + i)
        left = term(3)
        b_left[i, 64:128] = left[64:].astype(BF16)
        send(b_left.at[i], from_right.at[i, 0:128], x_down, bx_down + i)
        keep_right[i] = right[64:]
        keep_left[i] = left[:64]
        keep_own[i] = term(0)

    def b_forward(i):
        wait(from_left.at[i, 0:128], bx_up + i)
        sum_right[i] = (keep_right[i] + from_left[i, 0:64].astype(F32)).astype(BF16)
        send(sum_right.at[i], from_left.at[i, 128:192], x_up, bx_up2 + i)
        wait(from_right.at[i, 0:128], bx_down + i)
        sum_left[i] = (keep_left[i] + from_right[i, 0:64].astype(F32)).astype(BF16)
        send(sum_left.at[i], from_right.at[i, 128:192], x_down, bx_down2 + i)

    def b_finish(i):
        if i >= DIRECT:
            whole = keep_own[i]
            for r, sem in ((1, bx_up), (3, bx_down), (2, bx_far)):
                wait(x_in.at[i, r], sem + i)
                whole = whole + x_in[i, r].astype(F32)
            top, low = whole[0:64], whole[64:128]
        else:
            top, low = b_ring_sum(i)
        row = lax.rem(z + ORDER[i], NY)
        hops = lax.rem(row - y + NY, NY)

        @pl.when(hops == 0)
        def _():
            grad_own[0:64] = top
            grad_own[64:128] = low

        away = hops != 0

        @pl.when(away)
        def _():
            row_out[i, 0:64] = top.astype(BF16)
            row_out[i, 64:128] = low.astype(BF16)
            send(row_out.at[i], row_in.at[hops], at_y(row), by_recv + hops, by_send + i, away, (row_in, i))

    def b_ring_sum(i):
        wait(from_left.at[i, 128:192], bx_up2 + i)
        wait(from_right.at[i, 128:192], bx_down2 + i)
        top = keep_own[i, 0:64] + from_left[i, 64:128].astype(F32) + from_right[i, 128:192].astype(F32)
        low = keep_own[i, 64:128] + from_left[i, 128:192].astype(F32) + from_right[i, 64:128].astype(F32)
        return top, low

    def rows_in(*steps):
        for i in steps:
            cot_sibling(ORDER[i])
            b_terms(i)

    kv_sem, kvx, kvy = new(4), new(NX), new(8)
    half_own = lax.rem(z, 2)

    def rotate_back(value):
        return value * cos_s[...] + pltpu.roll(value, HD // 2, 1) * sin_s[...]

    def backward():
        grad = grad_own[...]
        for j in range(1, NY):
            wait(row_in.at[j], by_recv + j)
            grad = grad + row_in[j].astype(F32)
        grad_b = grad.astype(BF16)
        kept = []
        for h in range(2):
            grad_h = grad_b[:, h * HD : (h + 1) * HD]
            probs = probs_s[h]
            prob_grad = dot_nt(grad_h, v_s[...])
            row_dot = jnp.sum(grad_h.astype(F32) * att_s[h], axis=1, keepdims=True)
            score_grad = (probs * (prob_grad - row_dot)).astype(BF16)
            query_post = dot_nn(score_grad, k_s[...]) * scale
            q_all[0, x, :, h * HD : (h + 1) * HD] = rotate_back(query_post).astype(BF16)
            kept.append((grad_h, score_grad))
        d_receive(0)
        key_post = jnp.zeros((PACK, HD), F32)
        value_post = jnp.zeros((PACK, HD), F32)
        for h, (grad_h, score_grad) in enumerate(kept):
            key_post = key_post + dot_tn(score_grad, q_s[:, h * HD : (h + 1) * HD]) * scale
            value_post = value_post + dot_nn(probs_t[h], grad_h)
        key_sum = rotate_back(key_post).astype(BF16)
        value_sum = value_post.astype(BF16)
        packed = dot_nn(key_sum, select[0]) + dot_nn(value_sum, select[1])
        kv_out[0] = packed[:, :HD].astype(BF16)
        kv_out[1] = packed[:, HD:].astype(BF16)
        send(kv_out.at[half_own], kv_in.at[1], sibling, kv_sem + 1)
        send(kv_out.at[1 - half_own], kv_in.at[2], pair_same, kv_sem + 2)
        send(kv_out.at[1 - half_own], kv_in.at[3], pair_other, kv_sem + 3)

    def key_value():
        kv_total = kv_out[half_own].astype(F32)
        for j in range(1, 4):
            wait(kv_in.at[j], kv_sem + j)
            kv_total = kv_total + kv_in[j].astype(F32)
        kv_total = jnp.where(c == 1, pltpu.roll(kv_total, HD // 2, 1), kv_total)
        low_lane = lax.broadcasted_iota(jnp.int32, (32, HD), 1) < HD // 2
        for j in range(2):
            part = jnp.where(
                low_lane,
                kv_total[64 * j : 64 * j + 32],
                pltpu.roll(kv_total[64 * j + 32 : 64 * j + 64], HD // 2, 1),
            )
            kv_all[0, x, :, j * HD : (j + 1) * HD] = part.astype(BF16)
        for j in (1, 3, 2):
            send(kv_all.at[0, x], kv_all.at[0, x], at_x(x + j), kvx + j)

    def kv_y_start():
        for j in range(1, NX):
            wait(kv_all.at[0, lax.rem(x + NX - j, NX)], kvx + j)
        for j in ORDER[1:5]:
            send(kv_all.at[0], kv_all.at[8 - j], at_y(y + j), kvy + 8 - j)

    dx_up, dx_down, dx_up2, dx_down2 = new(8), new(8), new(8), new(8)
    head, tail = pl.ds(0, 64), pl.ds(64, 64)

    dy = new(8)

    dy_far, kvy_far = new(2), new(2)

    def far_along_y(buf, parts, sem, sem_far, o):
        if o in (1, 7):
            to = 3 if o == 1 else 5
            dev = at_y(y + 6) if o == 1 else at_y(y + 2)
            send(buf(o), buf(to), dev, sem + to)
        elif o in (2, 6):
            k = 1 if o == 2 else 0
            dev = at_y(y + 6) if o == 2 else at_y(y + 2)
            send(buf(o).at[parts[k]], buf(4).at[parts[k]], dev, sem_far + k)

    def wait_along_y(buf, parts, sem, sem_far, o):
        if o == 4:
            for k in range(2):
                wait(buf(4).at[parts[k]], sem_far + k)
        elif o:
            wait(buf(o), sem + o)

    def d_receive(*steps):
        for i in steps:
            o = ORDER[i]
            mine = q_all.at[o, x]
            q_at = (lambda r: q_all.at[r, x], (head, tail), dy, dy_far, o)
            wait_along_y(*q_at)
            far_along_y(*q_at)
            send(mine, mine, x_up, dx_up + i)
            send(mine, mine, x_down, dx_down + i)
            if o == 0:
                for j in ORDER[1:5]:
                    send(mine, q_all.at[8 - j, x], at_y(y + j), dy + 8 - j)

    def kv_far(*offsets):
        for o in offsets:
            kv_at = (lambda r: kv_all.at[r], (pl.ds(0, 2), pl.ds(2, 2)), kvy, kvy_far, o)
            wait_along_y(*kv_at)
            far_along_y(*kv_at)

    def d_forward(*steps):
        for i in steps:
            o = ORDER[i]
            wait(q_all.at[o, x_m], dx_up + i)
            send(q_all.at[o, x_m, head], q_all.at[o, x_m, head], x_up, dx_up2 + i)
            wait(q_all.at[o, x_p], dx_down + i)
            send(q_all.at[o, x_p, tail], q_all.at[o, x_p, tail], x_down, dx_down2 + i)

    sib_sem = new(8)

    def unpack(o, xx):
        raw = kv_all[o, xx].astype(F32)
        parts = []
        for j in range(2):
            part = raw[:, j * HD : (j + 1) * HD]
            parts += [part, pltpu.roll(part, HD // 2, 1)]
        return jnp.concatenate(parts, axis=0).astype(BF16)

    def d_terms(*steps):
        for i in steps:
            o = ORDER[i]
            wait(q_all.at[o, x_2, head], dx_up2 + i)
            wait(q_all.at[o, x_2, tail], dx_down2 + i)
            if o in (3, 4, 5):
                kv_far(o)
            for xx in range(NX):
                kv_rows[o, xx] = unpack(o, xx)
            for own in (False, True):
                cc = c if own else 1 - c
                rows = dot_nt(q_all[o, pl.ds(2 * cc, 2)].reshape(BLOCK, BLOCK), wq_s[...])
                rows = rows + dot_nn(kv_rows[o, pl.ds(2 * cc, 2)].reshape(BLOCK, HD), w_kv[...])
                if own:
                    term_own[i] = rows
                else:
                    sib_out[i] = rows.astype(BF16)
                    send(sib_out.at[i], sib_in.at[i], sibling, sib_sem + i)

    def weights(*steps):
        for i in steps:
            o = ORDER[i]
            oz = lax.rem(y + o - z + NZ, NZ)
            for cc in range(2):
                acts = in_all[oz, cc]
                q_acc[...] += dot_nn(acts, q_all[o, 2 * cc : 2 * cc + 2].reshape(BLOCK, BLOCK))
                kv_acc[...] += dot_nn(acts, kv_rows[o, 2 * cc : 2 * cc + 2].reshape(BLOCK, HD))

    chain_send = new(16)
    chain_recv = new(64)
    halves = (pl.ds(0, PACK), pl.ds(PACK, PACK))

    def f_place(i):
        hops = lax.rem(y + ORDER[i] - z + NZ, NZ)
        return hops, (hops > 4).astype(jnp.int32)

    def f_send(i, slot, k, dev, order):
        part = pl.ds(pl.multiple_of(k * PACK, PACK), PACK)
        copy_of(
            chain_out.at[i, part],
            chain_in.at[i, slot, part],
            dev,
            chain_send + 2 * i + order,
            chain_recv + 8 * i + 2 * slot + k,
        ).start()

    def f_wait(i, slot, k):
        part = pl.ds(pl.multiple_of(k * PACK, PACK), PACK)
        wait(chain_in.at[i, slot, part], chain_recv + 8 * i + 2 * slot + k)
        return chain_in[i, slot, part, :].astype(F32)

    def f_sibling(*steps):
        for i in steps:
            f_first(i)

    def f_first(i):
        wait(sib_in.at[i], sib_sem + i)
        hops, side = f_place(i)
        total = term_own[i] + sib_in[i].astype(F32)
        term_own[i] = total

        @pl.when((hops != 0) & (hops != 2) & (hops != 6))
        def _():
            chain_out[i] = total.astype(BF16)

        @pl.when(hops == 4)
        def _():
            f_send(i, 1, 0, at_z(z + 2), 0)
            f_send(i, 1, 1, at_z(z + NZ - 2), 1)

        @pl.when((hops == 1) | (hops == 3) | (hops == 5) | (hops == 7))
        def _():
            slot = (hops == 7).astype(jnp.int32)
            for k in range(2):
                f_send(i, slot, k, at_z(z + 1 + side * (NZ - 2)), k)

    def f_middle(*steps):
        for i in steps:
            f_second(i)

    def f_second(i):
        hops, side = f_place(i)

        @pl.when((hops == 2) | (hops == 6))
        def _():
            for order in range(2):
                k = side if order == 0 else 1 - side
                part = pl.ds(pl.multiple_of(k * PACK, PACK), PACK)
                total = term_own[i, part, :] + f_wait(i, 0, k)
                if order == 0:
                    total = total + f_wait(i, 1, k)
                chain_out[i, part, :] = total.astype(BF16)
                f_send(i, 2 + side, k, at_z(z + 2 + side * (NZ - 4)), order)

    def f_owner(*steps):
        for i in steps:
            f_last(i)

    def f_last(i):
        hops, _ = f_place(i)

        @pl.when(hops == 0)
        def _():
            for k in range(2):
                total = term_own[i, halves[k], :]
                for slot in range(4):
                    total = total + f_wait(i, slot, k)
                fin[halves[k], :] = total

    def f_drain(i):
        hops, _ = f_place(i)

        @pl.when(hops != 0)
        def _():
            for k in range(2):
                like = chain_out.at[i, halves[k]]
                copy_of(like, like, sibling, chain_send + 2 * i + k, chain_recv).wait_send()

    def o_compute(*offsets):
        total = o_acc[...]
        for o in offsets:
            oz = lax.rem(y + o - z + NZ, NZ)
            for xx in range(NX):
                sub = (xx % 2) * PACK
                total = total + dot_nn(att_all[o, xx, 0 : 2 * HD, :], cot_all[oz, xx // 2, sub : sub + PACK, :])
        o_acc[...] = total

    loads[6].wait()
    rows_in(0)
    cot_step(1)
    tables()
    att_y_start()
    rows_in(1, 2)
    cot_step(2)
    b_forward(0)
    rows_in(3, 4)
    att_y_step(1, 0)
    cot_step(3)
    b_forward(1)
    b_forward(2)
    b_finish(0)
    att_y_step(1, 1)
    rows_in(5, 6)
    cot_step(4)
    in_start()
    att_y_step(2, 0)
    b_forward(3)
    b_forward(4)
    b_finish(1)
    b_finish(2)
    b_forward(5)
    b_forward(6)
    rows_in(7)
    b_finish(3)
    b_finish(4)
    in_step(1)
    b_finish(5)
    b_finish(6)
    b_finish(7)
    backward()
    key_value()
    d_receive(1, 2)
    d_forward(0)
    kv_y_start()
    in_step(2)
    d_receive(3, 4)
    d_forward(1, 2)
    kv_far(1, 7)
    d_receive(5, 6)
    d_terms(0)
    kv_far(2, 6)
    in_step(3)
    d_forward(3, 4)
    d_receive(7)
    d_terms(1, 2)
    f_sibling(0)
    d_forward(5, 6)
    att_y_step(2, 1)
    d_terms(3, 4)
    d_forward(7)
    in_step(4)
    f_sibling(1, 2)
    att_y_step(3, 0)
    d_terms(5, 6)
    f_sibling(3, 4)
    d_terms(7)
    f_middle(0, 1, 2)
    f_sibling(5, 6)
    f_sibling(7)
    att_y_step(3, 1)
    for o in range(8):
        in_sibling(o)
    f_middle(3, 4)
    f_middle(5, 6)
    f_middle(7)
    weights(0, 1, 2, 3, 4, 5, 6, 7)
    o_compute(0, 1, 7, 2, 6, 3, 5)
    f_owner(0, 1, 2, 3, 4, 5, 6)
    att_y_step(4, 0)
    att_y_step(4, 1)
    o_compute(4)
    f_owner(7)

    total = jnp.zeros((16, PACK), F32)
    for o in range(8):
        for xx in range(NX):
            total = total + att_all[o, xx, 2 * HD : ATT_ROWS, :].astype(F32)
    inv = 1.0 / total[0:1, 0:1]
    gin_ref[...] = (fin[...] * inv).astype(BF16)
    gq_ref[...] = (q_acc[...] * inv).astype(BF16)
    kv_sum = kv_acc[...] * inv
    kv_cols = kv_sum.T
    gk_ref[...] = kv_cols[0:32].astype(BF16)
    gv_ref[...] = kv_cols[32:64].astype(BF16)
    go_ref[...] = (o_acc[...] * inv).astype(BF16)

    for copy, when in drain:
        if when is None:
            copy.wait_send()
        else:
            (buf, i), sem = copy

            @pl.when(when)
            def _():
                like = buf.at[i, 0:PACK]
                copy_of(like, like, sibling, sem, sem).wait_send()

    for i in range(8):
        f_drain(i)
    assert used[0] <= SEMS, used[0]


SEMS = 384


def hand_over(*refs):
    srcs, dsts, bufs, sems = refs[:5], refs[5:10], refs[10:15], refs[15]
    loads = [pltpu.make_async_copy(a, b, sems.at[0, i]) for i, (a, b) in enumerate(zip(srcs, bufs))]
    stores = [pltpu.make_async_copy(a, b, sems.at[1, i]) for i, (a, b) in enumerate(zip(bufs, dsts))]
    for load in loads:
        load.start()
    for load, store in zip(loads, stores):
        load.wait()
        store.start()
    for store in stores:
        store.wait()


def on_device(inputs, cotangent, queries, keys, values, lengths, counts, wq, wk, wv, wo):
    vmem = pl.BlockSpec(memory_space=pltpu.VMEM)
    hbm = pl.BlockSpec(memory_space=pltpu.HBM)
    sd = jax.ShapeDtypeStruct
    shapes = (
        sd((BLOCK, BLOCK), BF16),
        sd((BLOCK, BLOCK), BF16),
        sd((32, BLOCK), BF16),
        sd((32, BLOCK), BF16),
        sd((BLOCK, BLOCK), BF16),
    )
    results = pl.pallas_call(
        kernel,
        out_shape=shapes,
        in_specs=[hbm] * 11,
        out_specs=(vmem,) * 5,
        scratch_shapes=[
            pltpu.VMEM((8, 2, BLOCK, BLOCK), BF16),
            pltpu.VMEM((8, 2, BLOCK, BLOCK), BF16),
            pltpu.VMEM((8, NX, ATT_ROWS, PACK), BF16),
            pltpu.VMEM((8, NX, PACK, BLOCK), BF16),
            pltpu.VMEM((8, NX, 32, BLOCK), BF16),
            pltpu.VMEM((8, NX, PACK, HD), BF16),
            pltpu.VMEM((8, PACK, BLOCK), BF16),
            pltpu.VMEM((8, NX, PACK, BLOCK), BF16),
            pltpu.VMEM((8, PACK, BLOCK), BF16),
            pltpu.VMEM((8, PACK, BLOCK), BF16),
            pltpu.VMEM((8, 64, BLOCK), F32),
            pltpu.VMEM((8, 64, BLOCK), F32),
            pltpu.VMEM((8, PACK, BLOCK), F32),
            pltpu.VMEM((8, 192, BLOCK), BF16),
            pltpu.VMEM((8, 192, BLOCK), BF16),
            pltpu.VMEM((8, 64, BLOCK), BF16),
            pltpu.VMEM((8, 64, BLOCK), BF16),
            pltpu.VMEM((8, PACK, BLOCK), BF16),
            pltpu.VMEM((8, PACK, BLOCK), BF16),
            pltpu.VMEM((PACK, BLOCK), F32),
            pltpu.VMEM((2, PACK, PACK), F32),
            pltpu.VMEM((2, PACK, PACK), BF16),
            pltpu.VMEM((2, HD, BLOCK), BF16),
            pltpu.VMEM((2, PACK, HD), F32),
            pltpu.VMEM((PACK, HD), F32),
            pltpu.VMEM((PACK, HD), F32),
            pltpu.VMEM((2, PACK, HD), BF16),
            pltpu.VMEM((4, PACK, HD), BF16),
            pltpu.VMEM((HD, BLOCK), BF16),
            pltpu.VMEM((BLOCK, BLOCK), F32),
            pltpu.VMEM((BLOCK, HD), F32),
            pltpu.VMEM((BLOCK, BLOCK), F32),
            pltpu.VMEM((8, BLOCK, BLOCK), F32),
            pltpu.VMEM((8, BLOCK, BLOCK), BF16),
            pltpu.VMEM((8, BLOCK, BLOCK), BF16),
            pltpu.VMEM((8, BLOCK, BLOCK), BF16),
            pltpu.VMEM((8, 4, BLOCK, BLOCK), BF16),
            pltpu.VMEM((BLOCK, BLOCK), F32),
            pltpu.VMEM((BLOCK, BLOCK), BF16),
            pltpu.VMEM((PACK, BLOCK), BF16),
            pltpu.VMEM((PACK, HD), BF16),
            pltpu.VMEM((PACK, HD), BF16),
            pltpu.VMEM((BLOCK, BLOCK), BF16),
            pltpu.VMEM((BLOCK, BLOCK), BF16),
            pltpu.SMEM((1, DOCS), jnp.int32),
            pltpu.SMEM((1, 1), jnp.int32),
            pltpu.SemaphoreType.DMA((SEMS,)),
            pltpu.SemaphoreType.DMA((SEMS,)),
            pltpu.SemaphoreType.DMA((11,)),
        ],
        compiler_params=pltpu.CompilerParams(
            collective_id=0, has_side_effects=True, vmem_limit_bytes=60 * 1024 * 1024
        ),
        name="attention_block_backward",
    )(inputs, cotangent, queries, keys, values, lengths, counts.reshape(1, 1), wq, wk.T, wv.T, wo)
    gin, gq, gk, gv, go = pl.pallas_call(
        hand_over,
        out_shape=shapes,
        in_specs=[hbm] * 5,
        out_specs=(hbm,) * 5,
        scratch_shapes=[pltpu.VMEM(a.shape, a.dtype) for a in shapes] + [pltpu.SemaphoreType.DMA((2, 5))],
        compiler_params=pltpu.CompilerParams(vmem_limit_bytes=60 * 1024 * 1024),
        name="hand_over",
    )(*results)
    return gin, gq, gk.T, gv.T, go


def solution(mesh):
    return jax.shard_map(
        on_device,
        mesh=mesh,
        in_specs=(
            P("tensor", "dp"),
            P("tensor", "dp"),
            P("dp", "tensor"),
            P("dp", None),
            P("dp", None),
            P("dp", None),
            P("dp"),
            P("dp", "tensor"),
            P("dp", "tensor"),
            P("dp", "tensor"),
            P("tensor", "dp"),
        ),
        out_specs=(
            P("tensor", "dp"),
            P("dp", "tensor"),
            P("dp", "tensor"),
            P("dp", "tensor"),
            P("tensor", "dp"),
        ),
        check_vma=False,
    )
```
